32 devices in a mesh: section: 8 (over y, x, core), inner: 4 (over z).
Axes of the slice: x: 2, y: 2, z: 4, core: 2. Of those that a mesh axis runs over, the one named last changes fastest.
Arguments:
- tokens: bfloat16 [2, 128, 3072], P(None, 'section'), may hold values from -6 to 6
- norm_gain: float32 [3072], replicated, may hold values from 0.5 to 1.5
- router: bfloat16 [3072, 8], replicated, may hold values from -0.21875 to 0.21875
- expert_in: bfloat16 [8, 2, 1024, 3072], P('section', None, 'inner'), may hold values from -0.109375 to 0.109375
- expert_out: bfloat16 [8, 1024, 3072], P('section', 'inner'), may hold values from -0.375 to 0.375
- choices: int32 [2, 128, 2], P(None, 'section'), may hold values from 0 to 7, all different within a row; in each aligned block of 16 rows (0 to 15, 16 to 31, ..., all dimensions but the last counted through in order) at most 8 rows name the same one
Outputs:
- layer_outputs: bfloat16 [2, 128, 3072], P(None, 'section', 'inner')
The draws below stay inside these ranges and needn't reach their ends.
Inputs may be any that keep to these rules, and one draw needn't show every extreme that they name: `choices`: the two experts of a row differ; in each micro-batch the 16 rows of one section name any expert at most 8 times.
All inputs are finite; a program needn't handle non-finite values.
Results may differ from the reference program's by a relative error of at most 0.019.
Values may be sent and summed in bfloat16 or wider, within the bound.
No kernel may reach another device: no remote copies, remote signals or barrier semaphores. Data moves between devices by JAX's collectives and lax.ppermute only.
A program may use at most 128 MiB of HBM per device.

```python
import math
import jax
import jax.numpy as jnp
import numpy as np
from jax import lax

D = 3072
E = 8
HID_DEV = 256
R_SEC = 16
MICRO = 2
CAP = 8
SPE = 1
HID_SEC = 1024
FF_WIN = 1024
ROWS = 128
N_INNER = 4


def block_levels(key, shape, cuts, least, high):
    level = 1.0
    for dim, parts in cuts:
        draws = jax.random.uniform(jax.random.fold_in(jax.random.fold_in(key, 6), dim), (parts,), jnp.float32, least / len(cuts), high / len(cuts))
        level = level * jnp.repeat(jnp.exp(draws), shape[dim] // parts).reshape((-1,) + (1,) * (len(shape) - 1 - dim))
    return level


def assign_block(key, own, number, rows, amount, top, reach, lean):
    order = jax.random.permutation(key, amount)
    packed, ordinary = portions_of(amount, rows * top, reach, lean, True), portions_of(amount, rows * top, reach, lean, False)
    places = jnp.arange(amount)

    def named(lengths, turn):
        used = int((lengths > 0).sum())
        fixed = max(1, used // 4)
        moved = fixed + (places - fixed + turn * (used - fixed)) % max(1, amount - fixed)
        return jnp.zeros((amount,), jnp.int32).at[order[jnp.where(places < fixed, places, moved)]].set(jnp.asarray(lengths, jnp.int32))

    lengths = jnp.where(number % 4 == 0, named(packed, number // 4), named(ordinary, number - number // 4 - 1))
    mixed = jax.random.permutation(jax.random.fold_in(own, 3), amount)
    giver, sink = mixed[0:amount // 2 * 2:2], mixed[1:amount // 2 * 2:2]
    margin = jnp.minimum(lengths[giver] - 1, reach - lengths[sink]) // 2
    margin = jnp.where((giver == order[0]) | (sink == order[0]) | (lengths[sink] == 0), 0, jnp.maximum(margin, 0))
    moved = jax.random.randint(jax.random.fold_in(own, 4), (amount // 2,), 0, 1 << 20) % (margin + 1)
    lengths = lengths.at[giver].add(-moved).at[sink].add(moved)
    items = jnp.searchsorted(jnp.cumsum(lengths), jnp.arange(rows * top), side="right").astype(jnp.int32)
    listing = items.reshape(top, rows).T
    listing = listing[jax.random.permutation(jax.random.fold_in(own, 1), rows)]
    turn = jax.random.randint(jax.random.fold_in(own, 2), (rows, 1), 0, top)
    return jnp.take_along_axis(listing, (jnp.arange(top)[None, :] + turn) % top, axis=1)


def portions_of(count, total, bound, lean, full):
    loads = [(1 << 20) // math.isqrt(standing ** lean) + 1 for standing in range(1, count + 1)]
    largest = bound if full else min(bound, max(-(-total // count), total * loads[0] // sum(loads)))
    least = 1 if total - largest >= count - 1 else 0
    counts, surplus = [largest] + [least] * (count - 1), total - largest - least * (count - 1)
    while surplus > 0:
        candidates = [i for i in range(1, count) if counts[i] < largest] or [i for i in range(1, count) if counts[i] < bound]
        mass, remaining = sum([loads[i] for i in candidates]), surplus
        for i in candidates:
            addition = min(bound - counts[i], max(1, remaining * loads[i] // mass), surplus)
            counts[i] = counts[i] + addition
            surplus = surplus - addition
    return np.array(counts)


def gaussian(stream_key, dims, scale, most, pieces=(), kind=jnp.bfloat16):
    array = jax.random.normal(stream_key, dims, jnp.float32) * scale
    if len(pieces) > 0:
        array = block_levels(stream_key, dims, pieces, -0.22, 0.18) * array
    return jnp.clip(array, min=-most, max=most).astype(kind)


def setup_inputs(seed: int = 0) -> dict:
    streams_of = jax.random.split(jax.random.key(seed), 7)
    tokens = gaussian(streams_of[0], (MICRO, ROWS, D), 1.0, 6.0, ((1, 8),))
    norm_gain = jnp.clip(jax.random.uniform(streams_of[1], (D,), jnp.float32, 0.5, 1.5), 0.5, 1.5)
    router = gaussian(streams_of[2], (D, E), (D // 4) ** -0.5, 0.21875)
    expert_in = gaussian(streams_of[3], (E * SPE, 2, HID_SEC, D), D ** -0.5, 0.109375, ((0, 8), (2, 4)))
    expert_out = gaussian(streams_of[4], (E * SPE, HID_SEC, D), (FF_WIN // 4) ** -0.5, 0.375, ((0, 8), (1, 4)))
    choices_keys = jax.random.split(jax.random.fold_in(streams_of[5], 1), MICRO * ROWS // R_SEC)
    choices_turns = jax.random.permutation(jax.random.fold_in(streams_of[5], 3), MICRO * ROWS // R_SEC)
    choices = jax.vmap(lambda own, number: assign_block(jax.random.fold_in(streams_of[5], 2), own, number, R_SEC, E, 2, CAP, 2))(choices_keys, choices_turns).reshape((MICRO, ROWS, 2))
    return {"tokens": tokens, "norm_gain": norm_gain, "router": router, "expert_in": expert_in, "expert_out": expert_out, "choices": choices}


epsilon = 1e-05

def reference(tokens, norm_gain, router, expert_in, expert_out, choices):
    w_in_all = expert_in.reshape(E, SPE, 2, HID_SEC, D)
    w_out_all = expert_out.reshape(E, SPE * N_INNER, HID_DEV, D)
    expert_ids = jnp.arange(E, dtype=jnp.int32)
    results = []
    for micro_idx in range(MICRO):
        values = tokens[micro_idx].astype(jnp.float32)
        inv_rms = lax.rsqrt(lax.optimization_barrier(jnp.mean(values * values, axis=-1, keepdims=True)) + epsilon)
        normed = (values * inv_rms * norm_gain).astype(jnp.bfloat16)
        logits = jnp.dot(normed, router, preferred_element_type=jnp.float32)
        chosen = choices[micro_idx]
        first_hot = (chosen[:, 0:1] == expert_ids[None, :]).astype(jnp.float32)
        second_hot = (chosen[:, 1:2] == expert_ids[None, :]).astype(jnp.float32)
        lead_logit = lax.optimization_barrier(jnp.sum(logits * first_hot, axis=1, keepdims=True))
        trail_logit = lax.optimization_barrier(jnp.sum(logits * second_hot, axis=1, keepdims=True))
        weight_a = 1.0 / (1.0 + jnp.exp(trail_logit - lead_logit))
        weight_b = 1.0 / (1.0 + jnp.exp(lead_logit - trail_logit))
        mixing = weight_a * first_hot + weight_b * second_hot
        normed_wide = normed.astype(jnp.float32)

        def expert_step(total, expert):
            w_in_e = lax.dynamic_index_in_dim(w_in_all, expert, 0, keepdims=False)
            w_out_e = lax.dynamic_index_in_dim(w_out_all, expert, 0, keepdims=False)
            gate_up = jnp.einsum('rd,jkfd->rjkf', normed_wide, w_in_e.astype(jnp.float32))
            active = (jax.nn.silu(gate_up[:, :, 0]) * gate_up[:, :, 1]).astype(jnp.bfloat16)
            active = active.reshape(ROWS, SPE * N_INNER, HID_DEV)

            def block_step(accum, block):
                act_block = lax.dynamic_index_in_dim(active, block, 1, keepdims=False)
                w_block = lax.dynamic_index_in_dim(w_out_e, block, 0, keepdims=False)
                part_out = jnp.dot(act_block, w_block, preferred_element_type=jnp.float32).astype(jnp.bfloat16)
                return (accum + part_out.astype(jnp.float32), None)
            expert_rows, _ = lax.scan(block_step, jnp.zeros((ROWS, D), jnp.float32), jnp.arange(SPE * N_INNER, dtype=jnp.int32))
            weight = lax.dynamic_index_in_dim(mixing, expert, 1, keepdims=True)
            return (total + weight * expert_rows, None)
        total, _ = lax.scan(expert_step, jnp.zeros((ROWS, D), jnp.float32), expert_ids)
        results.append((values + total).astype(jnp.bfloat16))
    return jnp.stack(results)
```

```python
import jax
import jax.numpy as jnp
from jax import lax
from jax.sharding import PartitionSpec as P

epsilon = 1e-05


def trade(value, axis, distance):
    count = lax.axis_size(axis)
    return lax.ppermute(value, axis, [(place, place ^ distance) for place in range(count)])


def mixing_of(normed, first, second, router, expert):
    logits = jnp.dot(normed, router, preferred_element_type=jnp.float32)
    ids = jnp.arange(router.shape[1], dtype=jnp.int32).astype(jnp.float32)
    first_hot = (first == ids[None, :]).astype(jnp.float32)
    second_hot = (second == ids[None, :]).astype(jnp.float32)
    lead = jnp.sum(logits * first_hot, axis=1, keepdims=True)
    trail = jnp.sum(logits * second_hot, axis=1, keepdims=True)
    weight_a = 1.0 / (1.0 + jnp.exp(trail - lead))
    weight_b = 1.0 / (1.0 + jnp.exp(lead - trail))
    mine = expert.astype(jnp.float32)
    return jnp.where(first == mine, weight_a, 0.0) + jnp.where(second == mine, weight_b, 0.0)


def body(tokens, norm_gain, router, expert_in, expert_out, choices):
    sections = lax.axis_size("section")
    inner_count = lax.axis_size("inner")
    member = lax.axis_index("inner")
    section = lax.axis_index("section")
    chips = sections // 2
    expert = section // (sections // router.shape[1])
    micro, row_count, width = tokens.shape
    rows = micro * row_count
    part = width // inner_count
    hidden = expert_in.shape[2]
    stacked_in = expert_in[0].reshape(2 * hidden, width)
    down = expert_out[0]

    own = tokens.reshape(rows, width)
    named = choices.reshape(rows, 2).astype(jnp.bfloat16)
    message = jnp.concatenate([own, named, jnp.zeros((rows, 126), jnp.bfloat16)], axis=1)
    here = jnp.stack([message] + [trade(message, "section", 2 * k) for k in range(1, chips)])
    there = trade(here, "section", 1)
    every = jnp.concatenate([here, there], axis=0).reshape(sections * rows, width + 128)

    values = every[:, :width].astype(jnp.float32)
    inv_rms = lax.rsqrt(jnp.mean(values * values, axis=-1, keepdims=True) + epsilon)
    normed = (values * inv_rms * norm_gain).astype(jnp.bfloat16)
    first = every[:, width : width + 1].astype(jnp.float32)
    second = every[:, width + 1 : width + 2].astype(jnp.float32)
    weight = mixing_of(normed, first, second, router, expert)
    gate_up = lax.dot_general(
        normed, stacked_in, (((1,), (1,)), ((), ())), preferred_element_type=jnp.float32
    )
    active = (jax.nn.silu(gate_up[:, :hidden]) * gate_up[:, hidden:]).astype(jnp.bfloat16)
    partial = jnp.dot(active, down, preferred_element_type=jnp.float32)
    weighted = (partial * weight).astype(jnp.bfloat16).reshape(2, chips, rows, width)
    back = trade(weighted[1], "section", 1)
    paired = (weighted[0].astype(jnp.float32) + back.astype(jnp.float32)).astype(jnp.bfloat16)
    total = paired[0].astype(jnp.float32)
    for k in range(1, chips):
        total = total + trade(paired[k], "section", 2 * k).astype(jnp.float32)
    mine = lax.dynamic_slice_in_dim(total, member * part, part, 1)
    rounded = total.astype(jnp.bfloat16)
    for k in range(1, inner_count):
        away = lax.dynamic_slice_in_dim(rounded, (member ^ k) * part, part, 1)
        mine = mine + trade(away, "inner", k).astype(jnp.float32)
    residual = lax.dynamic_slice_in_dim(own, member * part, part, 1).astype(jnp.float32)
    return (residual + mine).astype(jnp.bfloat16).reshape(micro, row_count, part)


def solution(mesh):
    return jax.shard_map(
        body,
        mesh=mesh,
        in_specs=(
            P(None, "section", None),
            P(),
            P(),
            P("section", None, "inner", None),
            P("section", "inner", None),
            P(None, "section", None),
        ),
        out_specs=P(None, "section", "inner"),
        check_vma=False,
    )
```

```python
import functools

import jax
import jax.numpy as jnp
from jax import lax
from jax.experimental import pallas as pl
from jax.experimental.pallas import tpu as pltpu
from jax.sharding import PartitionSpec as P

epsilon = 1e-05
LANES = 128
NT = (((1,), (1,)), ((), ()))
VMEM = pl.BlockSpec(memory_space=pltpu.VMEM)
HBM = pl.BlockSpec(memory_space=pltpu.HBM)
SMEM = pl.BlockSpec(memory_space=pltpu.SMEM)
PARAMS = pltpu.CompilerParams(vmem_limit_bytes=20 * 1024 * 1024)


def trade(value, axis, distance):
    count = lax.axis_size(axis)
    return lax.ppermute(value, axis, [(place, place ^ distance) for place in range(count)])


def shaped(rows, width, dtype):
    return jax.ShapeDtypeStruct((rows, width), dtype)


def expert_at(section, distance, per_expert):
    return lax.div(section ^ (2 * distance), jnp.int32(per_expert))


def pack_kernel(chips, per_expert, experts, section_ref, tokens_ref, other_ref, named_ref, other_named_ref, gain_ref, *refs):
    out_refs, normed_ref, slots_ref, named_rows_ref = refs[:chips], refs[chips], refs[chips + 1], refs[chips + 2]
    micro, _, row_count = named_ref.shape
    rows = tokens_ref.shape[0]
    for place, ref in enumerate((tokens_ref, other_ref)):
        values = ref[...].astype(jnp.float32)
        inv_rms = lax.rsqrt(jnp.mean(values * values, axis=-1, keepdims=True) + epsilon)
        normed_ref[place * rows : (place + 1) * rows, :] = (
            values * inv_rms * gain_ref[...]
        ).astype(jnp.bfloat16)
    named = [
        jnp.concatenate(
            [ref[m, k : k + 1, :] for ref in (named_ref, other_named_ref) for m in range(micro)],
            axis=1,
        ).astype(jnp.float32)
        for k in range(2)
    ]
    every = 2 * rows
    capacity = row_count // 2
    ids = lax.broadcasted_iota(jnp.int32, (experts, every), 0).astype(jnp.float32)
    hit = (named[0] == ids) | (named[1] == ids)
    above = lax.broadcasted_iota(jnp.int32, (every, every), 0)
    column = lax.broadcasted_iota(jnp.int32, (every, every), 1)
    earlier = (above < column) & (above // row_count == column // row_count)
    rank = jnp.dot(
        hit.astype(jnp.bfloat16), earlier.astype(jnp.bfloat16), preferred_element_type=jnp.float32
    )
    group = lax.broadcasted_iota(jnp.int32, (experts, every), 1) // row_count
    slots = jnp.where(hit, (group * capacity).astype(jnp.float32) + rank, -1.0)
    slots_ref[...] = slots
    named_rows_ref[0:1, :] = named[0]
    named_rows_ref[1:2, :] = named[1]
    section = section_ref[0]
    slot_ids = lax.broadcasted_iota(jnp.int32, (rows, every), 0).astype(jnp.float32)
    picks = []
    for k in range(chips):
        expert = expert_at(section, k, per_expert).astype(jnp.float32)
        slot = jnp.sum(jnp.where(ids == expert, slots, 0.0), axis=0, keepdims=True)
        picks.append(jnp.where(slot == slot_ids, 1.0, 0.0))
    pick = jnp.concatenate(picks, axis=0).astype(jnp.bfloat16)
    packed = jnp.dot(pick, normed_ref[...], preferred_element_type=jnp.float32)
    for k, out_ref in enumerate(out_refs):
        out_ref[...] = packed[k * rows : (k + 1) * rows, :].astype(jnp.bfloat16)


def pack(section, tokens, other, named, other_named, gain, chips, per_expert, experts):
    rows, width = tokens.shape
    return pl.pallas_call(
        functools.partial(pack_kernel, chips, per_expert, experts),
        out_shape=[shaped(rows, width, jnp.bfloat16)] * chips
        + [
            shaped(2 * rows, width, jnp.bfloat16),
            shaped(experts, 2 * rows, jnp.float32),
            shaped(2, 2 * rows, jnp.float32),
        ],
        in_specs=[SMEM] + [VMEM] * 5,
        out_specs=[VMEM] * (chips + 3),
        compiler_params=PARAMS,
        name="pack",
    )(section, tokens, other, named, other_named, gain)


def mix_kernel(sets, per_expert, section_ref, normed_ref, slots_ref, named_ref, router_ref, *outs):
    experts, every = slots_ref.shape
    rows = every // 2
    logits = lax.dot_general(
        normed_ref[...], router_ref[...], NT, preferred_element_type=jnp.float32
    )
    diagonal = lax.broadcasted_iota(jnp.int32, (every, every), 0) == (
        lax.broadcasted_iota(jnp.int32, (every, every), 1)
    )

    def upright(row):
        return jnp.sum(jnp.where(diagonal, row, 0.0), axis=1, keepdims=True)

    first, second = upright(named_ref[0:1, :]), upright(named_ref[1:2, :])
    ids = lax.broadcasted_iota(jnp.int32, logits.shape, 1).astype(jnp.float32)
    lead = jnp.sum(jnp.where(first == ids, logits, 0.0), axis=1, keepdims=True)
    trail = jnp.sum(jnp.where(second == ids, logits, 0.0), axis=1, keepdims=True)
    weight_a = 1.0 / (1.0 + jnp.exp(trail - lead))
    weight_b = 1.0 / (1.0 + jnp.exp(lead - trail))
    section = section_ref[0]
    tall = lax.broadcasted_iota(jnp.int32, (experts, every), 0).astype(jnp.float32)
    for place, ks in enumerate(sets):
        shape = (every, len(ks) * rows)
        lanes = lax.broadcasted_iota(jnp.int32, shape, 1).astype(jnp.float32)
        spread = jnp.zeros(shape, jnp.float32)
        for at, k in enumerate(ks):
            expert = expert_at(section, k, per_expert).astype(jnp.float32)
            slot = jnp.sum(jnp.where(tall == expert, slots_ref[...], 0.0), axis=0, keepdims=True)
            weight = jnp.where(first == expert, weight_a, 0.0) + jnp.where(
                second == expert, weight_b, 0.0
            )
            spread = spread + jnp.where(upright(slot) + at * rows == lanes, weight, 0.0)
        high = spread.astype(jnp.bfloat16)
        outs[2 * place][...] = high
        outs[2 * place + 1][...] = (spread - high.astype(jnp.float32)).astype(jnp.bfloat16)


def mix(section, normed, slots, named, router, sets, per_expert):
    every = normed.shape[0]
    shapes = [shaped(every, len(ks) * every // 2, jnp.bfloat16) for ks in sets for _ in range(2)]
    return pl.pallas_call(
        functools.partial(mix_kernel, sets, per_expert),
        out_shape=shapes,
        in_specs=[SMEM] + [VMEM] * 4,
        out_specs=[VMEM] * len(shapes),
        compiler_params=PARAMS,
        name="mix",
    )(section, normed, slots, named, router)


def fetch_kernel(count, *refs):
    sources, targets, sems = refs[:count], refs[-1 - count : -1], refs[-1]
    copies = [
        pltpu.make_async_copy(source, target, sems.at[k])
        for k, (source, target) in enumerate(zip(sources, targets))
    ]
    for copy in copies:
        copy.start()
    for copy in copies:
        copy.wait()


def fetch(arrays, after=()):
    count = len(arrays)
    return pl.pallas_call(
        functools.partial(fetch_kernel, count),
        out_shape=[jax.ShapeDtypeStruct(a.shape, a.dtype) for a in arrays],
        in_specs=[HBM] * count + [VMEM] * len(after),
        out_specs=[VMEM] * count,
        scratch_shapes=[pltpu.SemaphoreType.DMA((count,))],
        compiler_params=PARAMS,
        name="fetch",
    )(*[pltpu.with_memory_space_constraint(a, pltpu.HBM) for a in arrays], *after)


def expert_kernel(count, in_ref, down_ref, *refs):
    blocks, out_refs, every_ref = refs[:count], refs[-1 - count : -1], refs[-1]
    rows = blocks[0].shape[0]
    for place, block in enumerate(blocks):
        every_ref[place * rows : (place + 1) * rows, :] = block[...]
    gate_up = lax.dot_general(
        every_ref[...], in_ref[...], NT, preferred_element_type=jnp.float32
    )
    hidden = gate_up.shape[1] // 2
    gate = gate_up[:, :hidden]
    active = (gate / (1.0 + jnp.exp(-gate)) * gate_up[:, hidden:]).astype(jnp.bfloat16)
    partial = jnp.dot(active, down_ref[...], preferred_element_type=jnp.float32)
    for place, out_ref in enumerate(out_refs):
        out_ref[...] = partial[place * rows : (place + 1) * rows, :].astype(jnp.bfloat16)


def run_expert(blocks, stacked_in, down, after=()):
    count = len(blocks)
    rows, width = blocks[0].shape
    return pl.pallas_call(
        functools.partial(expert_kernel, count),
        out_shape=[shaped(rows, width, jnp.bfloat16)] * count,
        in_specs=[VMEM] * (2 + count) + [pl.BlockSpec(memory_space=pl.ANY)] * len(after),
        out_specs=[VMEM] * count,
        scratch_shapes=[pltpu.VMEM((count * rows, width), jnp.bfloat16)],
        compiler_params=PARAMS,
        name="expert",
    )(stacked_in, down, *blocks, *after)


def gathered(blocks, every_ref):
    rows = blocks[0].shape[0]
    for place, block in enumerate(blocks):
        every_ref[place * rows : (place + 1) * rows, :] = block[...]
    return every_ref[...]


def begin_kernel(count, high_ref, low_ref, *refs):
    blocks, out_ref, every_ref = refs[:count], refs[count], refs[-1]
    every = gathered(blocks, every_ref)
    total = jnp.dot(low_ref[...], every, preferred_element_type=jnp.float32)
    out_ref[...] = total + jnp.dot(high_ref[...], every, preferred_element_type=jnp.float32)


def begin(high, low, blocks):
    count = len(blocks)
    rows, width = blocks[0].shape
    return pl.pallas_call(
        functools.partial(begin_kernel, count),
        out_shape=shaped(2 * rows, width, jnp.float32),
        in_specs=[VMEM] * (2 + count),
        out_specs=VMEM,
        scratch_shapes=[pltpu.VMEM((count * rows, width), jnp.bfloat16)],
        compiler_params=PARAMS,
        name="begin",
    )(high, low, *blocks)


def combine_kernel(count, high_ref, low_ref, begun_ref, *refs):
    blocks, keep_ref, send_ref, every_ref = refs[:count], refs[count], refs[count + 1], refs[-1]
    rows = blocks[0].shape[0]
    every = gathered(blocks, every_ref)
    total = begun_ref[...] + jnp.dot(low_ref[...], every, preferred_element_type=jnp.float32)
    total = total + jnp.dot(high_ref[...], every, preferred_element_type=jnp.float32)
    keep_ref[...] = total[:rows]
    send_ref[...] = total[rows:].astype(jnp.bfloat16)


def combine(high, low, begun, blocks):
    count = len(blocks)
    rows, width = blocks[0].shape
    return pl.pallas_call(
        functools.partial(combine_kernel, count),
        out_shape=[shaped(rows, width, jnp.float32), shaped(rows, width, jnp.bfloat16)],
        in_specs=[VMEM] * (3 + count),
        out_specs=[VMEM] * 2,
        scratch_shapes=[pltpu.VMEM((count * rows, width), jnp.bfloat16)],
        compiler_params=PARAMS,
        name="combine",
    )(high, low, begun, *blocks)


def split_kernel(member_ref, tokens_ref, keep_ref, back_ref, *outs):
    part = outs[0].shape[1]
    for k, out_ref in enumerate(outs):
        columns = pl.ds(pl.multiple_of((member_ref[0] ^ k) * part, LANES), part)
        total = keep_ref[:, columns] + back_ref[:, columns].astype(jnp.float32)
        if k == 0:
            total = total + tokens_ref[:, columns].astype(jnp.float32)
        out_ref[...] = total.astype(out_ref.dtype)


def split_up(keep, back, tokens, member, inner_count):
    rows, width = keep.shape
    part = width // inner_count
    if part % LANES:
        total = keep + back.astype(jnp.float32)
        rounded = total.astype(jnp.bfloat16)
        total = total + tokens.astype(jnp.float32)
        outs = [lax.dynamic_slice_in_dim(total, member * part, part, 1)]
        for k in range(1, inner_count):
            outs.append(lax.dynamic_slice_in_dim(rounded, (member ^ k) * part, part, 1))
        return outs
    kinds = [jnp.float32] + [jnp.bfloat16] * (inner_count - 1)
    return pl.pallas_call(
        split_kernel,
        out_shape=[shaped(rows, part, kind) for kind in kinds],
        in_specs=[SMEM] + [VMEM] * 3,
        out_specs=[VMEM] * inner_count,
        compiler_params=PARAMS,
        name="split",
    )(member.reshape(1), tokens, keep, back)


def final_kernel(*refs):
    out_ref = refs[-1]
    micro, row_count, _ = out_ref.shape
    total = refs[0][...]
    for ref in refs[1:-1]:
        total = total + ref[...].astype(jnp.float32)
    for m in range(micro):
        out_ref[m] = total[m * row_count : (m + 1) * row_count].astype(out_ref.dtype)


def finish(pieces, micro, row_count):
    part = pieces[0].shape[1]
    return pl.pallas_call(
        final_kernel,
        out_shape=jax.ShapeDtypeStruct((micro, row_count, part), jnp.bfloat16),
        in_specs=[VMEM] * len(pieces),
        out_specs=VMEM,
        compiler_params=PARAMS,
        name="finish",
    )(*pieces)


def body(tokens, norm_gain, router, expert_in, expert_out, choices):
    sections = lax.axis_size("section")
    inner_count = lax.axis_size("inner")
    member = lax.axis_index("inner").astype(jnp.int32)
    section = lax.axis_index("section").astype(jnp.int32).reshape(1)
    chips = sections // 2
    experts = router.shape[1]
    per_expert = sections // experts
    micro, row_count, width = tokens.shape
    rows = micro * row_count
    hidden = expert_in.shape[2]
    own = tokens.reshape(rows, width)
    named = choices.transpose(0, 2, 1)
    gain = norm_gain.reshape(1, width)

    other = trade(own, "section", 1)
    other_named = trade(named, "section", 1)
    own, named, gain = fetch((own, named, gain))
    *messages, normed, slots, names = pack(
        section, own, other, named, other_named, gain, chips, per_expert, experts
    )
    order = list(range(1, chips))
    arrived = {k: trade(messages[k], "section", 2 * k) for k in reversed(order)}
    router_rows, stacked_in, down = fetch(
        (router.T, expert_in[0].reshape(2 * hidden, width), expert_out[0]), (slots,)
    )
    far, near = order[-1], order[:-1]
    sets = ((0, far), tuple(near))
    high_a, low_a, high_b, low_b = mix(
        section, normed, slots, names, router_rows, sets, per_expert
    )
    here, away = run_expert([messages[0], arrived[far]], stacked_in, down)
    early = [here, trade(away, "section", 2 * far)]
    late = run_expert([arrived[k] for k in near], stacked_in, down, (here,))
    late = [trade(value, "section", 2 * k) for k, value in zip(near, late)]
    begun = begin(high_a, low_a, early)
    keep, send = combine(high_b, low_b, begun, late)
    back = trade(send, "section", 1)
    split = split_up(keep, back, own, member, inner_count)
    pieces = {k: trade(split[k], "inner", k) for k in reversed(range(1, inner_count))}
    pieces[0] = split[0]
    return finish([pieces[k] for k in [0] + list(reversed(range(1, inner_count)))], micro, row_count)


def solution(mesh):
    return jax.shard_map(
        body,
        mesh=mesh,
        in_specs=(
            P(None, "section", None),
            P(),
            P(),
            P("section", None, "inner", None),
            P("section", "inner", None),
            P(None, "section", None),
        ),
        out_specs=P(None, "section", "inner"),
        check_vma=False,
    )
```

```python
import functools

import jax
import jax.numpy as jnp
from jax import lax
from jax.experimental import pallas as pl
from jax.experimental.pallas import tpu as pltpu
from jax.sharding import PartitionSpec as P

epsilon = 1e-05
LANES = 128
NT = (((1,), (1,)), ((), ()))
VMEM = pl.BlockSpec(memory_space=pltpu.VMEM)
ANY = pl.BlockSpec(memory_space=pl.ANY)
HBM = pl.BlockSpec(memory_space=pltpu.HBM)
SMEM = pl.BlockSpec(memory_space=pltpu.SMEM)
PARAMS = pltpu.CompilerParams(vmem_limit_bytes=20 * 1024 * 1024)


def trade(value, axis, distance):
    count = lax.axis_size(axis)
    return lax.ppermute(value, axis, [(place, place ^ distance) for place in range(count)])


def shaped(rows, width, dtype):
    return jax.ShapeDtypeStruct((rows, width), dtype)


def expert_at(section, distance, per_expert):
    return lax.div(section ^ distance, jnp.int32(per_expert))


def pack_kernel(chips, per_expert, experts, section_ref, tokens_ref, other_ref, named_ref, other_named_ref, gain_ref, *refs):
    out_refs, normed_ref, slots_ref, named_rows_ref = refs[:chips], refs[chips], refs[chips + 1], refs[chips + 2]
    micro, _, row_count = named_ref.shape
    rows = tokens_ref.shape[0]
    for place, ref in enumerate((tokens_ref, other_ref)):
        values = ref[...].astype(jnp.float32)
        inv_rms = lax.rsqrt(jnp.mean(values * values, axis=-1, keepdims=True) + epsilon)
        normed_ref[place * rows : (place + 1) * rows, :] = (
            values * inv_rms * gain_ref[...]
        ).astype(jnp.bfloat16)
    named = [
        jnp.concatenate(
            [ref[m, k : k + 1, :] for ref in (named_ref, other_named_ref) for m in range(micro)],
            axis=1,
        ).astype(jnp.float32)
        for k in range(2)
    ]
    every = 2 * rows
    capacity = row_count // 2
    ids = lax.broadcasted_iota(jnp.int32, (experts, every), 0).astype(jnp.float32)
    hit = (named[0] == ids) | (named[1] == ids)
    above = lax.broadcasted_iota(jnp.int32, (every, every), 0)
    column = lax.broadcasted_iota(jnp.int32, (every, every), 1)
    earlier = (above < column) & (above // row_count == column // row_count)
    rank = jnp.dot(
        hit.astype(jnp.bfloat16), earlier.astype(jnp.bfloat16), preferred_element_type=jnp.float32
    )
    group = lax.broadcasted_iota(jnp.int32, (experts, every), 1) // row_count
    slots = jnp.where(hit, (group * capacity).astype(jnp.float32) + rank, -1.0)
    slots_ref[...] = slots
    named_rows_ref[0:1, :] = named[0]
    named_rows_ref[1:2, :] = named[1]
    section = section_ref[0]
    slot_ids = lax.broadcasted_iota(jnp.int32, (rows, every), 0).astype(jnp.float32)
    picks = []
    for k in range(chips):
        expert = expert_at(section, 2 * k, per_expert).astype(jnp.float32)
        slot = jnp.sum(jnp.where(ids == expert, slots, 0.0), axis=0, keepdims=True)
        picks.append(jnp.where(slot == slot_ids, 1.0, 0.0))
    pick = jnp.concatenate(picks, axis=0).astype(jnp.bfloat16)
    packed = jnp.dot(pick, normed_ref[...], preferred_element_type=jnp.float32)
    for k, out_ref in enumerate(out_refs):
        out_ref[...] = packed[k * rows : (k + 1) * rows, :].astype(jnp.bfloat16)


def pack(section, tokens, other, named, other_named, gain, chips, per_expert, experts):
    rows, width = tokens.shape
    return pl.pallas_call(
        functools.partial(pack_kernel, chips, per_expert, experts),
        out_shape=[shaped(rows, width, jnp.bfloat16)] * chips
        + [
            shaped(2 * rows, width, jnp.bfloat16),
            shaped(experts, 2 * rows, jnp.float32),
            shaped(2, 2 * rows, jnp.float32),
        ],
        in_specs=[SMEM] + [VMEM] * 5,
        out_specs=[VMEM] * (chips + 3),
        compiler_params=PARAMS,
        name="pack",
    )(section, tokens, other, named, other_named, gain)


def mix_kernel(sets, per_expert, section_ref, normed_ref, slots_ref, named_ref, router_ref, *outs):
    experts, every = slots_ref.shape
    rows = every // 2
    logits = lax.dot_general(
        normed_ref[...], router_ref[...], NT, preferred_element_type=jnp.float32
    )
    diagonal = lax.broadcasted_iota(jnp.int32, (every, every), 0) == (
        lax.broadcasted_iota(jnp.int32, (every, every), 1)
    )

    def upright(row):
        return jnp.sum(jnp.where(diagonal, row, 0.0), axis=1, keepdims=True)

    first, second = upright(named_ref[0:1, :]), upright(named_ref[1:2, :])
    ids = lax.broadcasted_iota(jnp.int32, logits.shape, 1).astype(jnp.float32)
    lead = jnp.sum(jnp.where(first == ids, logits, 0.0), axis=1, keepdims=True)
    trail = jnp.sum(jnp.where(second == ids, logits, 0.0), axis=1, keepdims=True)
    weight_a = 1.0 / (1.0 + jnp.exp(trail - lead))
    weight_b = 1.0 / (1.0 + jnp.exp(lead - trail))
    section = section_ref[0]
    tall = lax.broadcasted_iota(jnp.int32, (experts, every), 0).astype(jnp.float32)
    for place, distances in enumerate(sets):
        high_ref, low_ref = outs[2 * place : 2 * place + 2]
        count, width = high_ref.shape
        each = width // len(distances)
        lanes = lax.broadcasted_iota(jnp.int32, (count, width), 1).astype(jnp.float32)
        spread = jnp.zeros((count, width), jnp.float32)
        for at, distance in enumerate(distances):
            expert = expert_at(section, distance, per_expert).astype(jnp.float32)
            slot = jnp.sum(jnp.where(tall == expert, slots_ref[...], 0.0), axis=0, keepdims=True)
            weight = jnp.where(first == expert, weight_a, 0.0) + jnp.where(
                second == expert, weight_b, 0.0
            )
            spread = spread + jnp.where(
                upright(slot)[:count] + at * each == lanes, weight[:count], 0.0
            )
        high = spread.astype(jnp.bfloat16)
        high_ref[...] = high
        low_ref[...] = (spread - high.astype(jnp.float32)).astype(jnp.bfloat16)


def mix(section, normed, slots, named, router, early, near, per_expert):
    every = normed.shape[0]
    rows = every // 2
    shapes = [
        shaped(rows, len(distances) * rows // 2, jnp.bfloat16)
        for distances in (early, near)
        for _ in range(2)
    ]
    return pl.pallas_call(
        functools.partial(mix_kernel, (early, near), per_expert),
        out_shape=shapes,
        in_specs=[SMEM] + [VMEM] * 4,
        out_specs=[VMEM] * len(shapes),
        compiler_params=PARAMS,
        name="mix",
    )(section, normed, slots, named, router)


def fetch_kernel(count, *refs):
    sources, targets, sems = refs[:count], refs[-1 - count : -1], refs[-1]
    copies = [
        pltpu.make_async_copy(source, target, sems.at[k])
        for k, (source, target) in enumerate(zip(sources, targets))
    ]
    for copy in copies:
        copy.start()
    for copy in copies:
        copy.wait()


def fetch(arrays, after=()):
    count = len(arrays)
    return pl.pallas_call(
        functools.partial(fetch_kernel, count),
        out_shape=[jax.ShapeDtypeStruct(a.shape, a.dtype) for a in arrays],
        in_specs=[HBM] * count + [VMEM] * len(after),
        out_specs=[VMEM] * count,
        scratch_shapes=[pltpu.SemaphoreType.DMA((count,))],
        compiler_params=PARAMS,
        name="fetch",
    )(*[pltpu.with_memory_space_constraint(a, pltpu.HBM) for a in arrays], *after)


def load_kernel(count, in_ref, *refs):
    sources, targets = refs[:count], refs[count + 2 : 2 * count + 2]
    turned_ref, held_ref, sems = refs[count + 1], refs[-2], refs[-1]
    pieces, rows, _ = held_ref.shape
    copies = [
        pltpu.make_async_copy(in_ref.at[pl.ds(k * rows, rows)], held_ref.at[k], sems.at[k])
        for k in range(pieces)
    ]
    others = [
        pltpu.make_async_copy(source, target, sems.at[pieces + k])
        for k, (source, target) in enumerate(zip(sources, targets))
    ]
    for copy in copies + others:
        copy.start()
    for k in range(pieces):
        copies[k].wait()
        turned_ref[:, k * rows : (k + 1) * rows] = held_ref[k].T
    for copy in others:
        copy.wait()


def load_weights(stacked_in, others, after):
    count = len(others)
    rows, width = stacked_in.shape
    pieces = max(1, rows // LANES)
    arrays = [stacked_in, *others]
    return pl.pallas_call(
        functools.partial(load_kernel, count),
        out_shape=[shaped(width, rows, stacked_in.dtype)]
        + [jax.ShapeDtypeStruct(a.shape, a.dtype) for a in others],
        in_specs=[HBM] * (count + 1) + [VMEM],
        out_specs=[VMEM] * (count + 1),
        scratch_shapes=[
            pltpu.VMEM((pieces, rows // pieces, width), stacked_in.dtype),
            pltpu.SemaphoreType.DMA((pieces + count,)),
        ],
        compiler_params=PARAMS,
        name="load_weights",
    )(*[pltpu.with_memory_space_constraint(a, pltpu.HBM) for a in arrays], after)


def expert_kernel(count, after, in_ref, down_ref, *refs):
    blocks, every_ref = refs[:count], refs[-1]
    out_refs = refs[count + after : -1]
    every = gathered(blocks, every_ref)
    gate_up = jnp.dot(every, in_ref[...], preferred_element_type=jnp.float32)
    hidden = gate_up.shape[1] // 2
    gate = gate_up[:, :hidden]
    active = (gate / (1.0 + jnp.exp(-gate)) * gate_up[:, hidden:]).astype(jnp.bfloat16)
    partial = jnp.dot(active, down_ref[...], preferred_element_type=jnp.float32)
    rows = out_refs[0].shape[0]
    for place, out_ref in enumerate(out_refs):
        out_ref[...] = partial[place * rows : (place + 1) * rows, :].astype(jnp.bfloat16)


def run_expert(blocks, turned_in, down, pieces, after=()):
    count = len(blocks)
    rows, width = blocks[0].shape
    return pl.pallas_call(
        functools.partial(expert_kernel, count, len(after)),
        out_shape=[shaped(rows // pieces, width, jnp.bfloat16)] * (count * pieces),
        in_specs=[VMEM] * (2 + count) + [ANY] * len(after),
        out_specs=[VMEM] * (count * pieces),
        scratch_shapes=[pltpu.VMEM((count * rows, width), jnp.bfloat16)],
        compiler_params=PARAMS,
        name="expert",
    )(turned_in, down, *blocks, *after)


def gathered(blocks, every_ref):
    rows = blocks[0].shape[0]
    for place, block in enumerate(blocks):
        every_ref[place * rows : (place + 1) * rows, :] = block[...]
    return every_ref[...]


def begin_kernel(count, high_ref, low_ref, *refs):
    blocks, out_ref, every_ref = refs[:count], refs[count], refs[-1]
    every = gathered(blocks, every_ref)
    total = jnp.dot(low_ref[...], every, preferred_element_type=jnp.float32)
    out_ref[...] = total + jnp.dot(high_ref[...], every, preferred_element_type=jnp.float32)


def begin(high, low, blocks):
    count = len(blocks)
    each, width = blocks[0].shape
    return pl.pallas_call(
        functools.partial(begin_kernel, count),
        out_shape=shaped(high.shape[0], width, jnp.float32),
        in_specs=[VMEM] * (2 + count),
        out_specs=VMEM,
        scratch_shapes=[pltpu.VMEM((count * each, width), jnp.bfloat16)],
        compiler_params=PARAMS,
        name="begin",
    )(high, low, *blocks)


def close_kernel(count, member_ref, tokens_ref, high_ref, low_ref, begun_ref, *refs):
    blocks, outs, every_ref, total_ref = refs[:count], refs[count:-2], refs[-2], refs[-1]
    every = gathered(blocks, every_ref)
    total = begun_ref[...] + jnp.dot(low_ref[...], every, preferred_element_type=jnp.float32)
    total_ref[...] = total + jnp.dot(high_ref[...], every, preferred_element_type=jnp.float32)
    if len(outs) == 1:
        outs[0][...] = total_ref[...]
        return
    part = outs[0].shape[1]
    for k, out_ref in enumerate(outs):
        columns = pl.ds(pl.multiple_of((member_ref[0] ^ k) * part, LANES), part)
        value = total_ref[:, columns]
        if k == 0:
            value = value + tokens_ref[:, columns].astype(jnp.float32)
        out_ref[...] = value.astype(out_ref.dtype)


def close(high, low, begun, blocks, tokens, member, inner_count):
    count = len(blocks)
    each = blocks[0].shape[0]
    rows, width = begun.shape
    part = width // inner_count
    whole = part % LANES != 0
    kinds = [jnp.float32] + [jnp.bfloat16] * (inner_count - 1)
    shapes = [shaped(rows, part, kind) for kind in kinds]
    if whole:
        shapes = [shaped(rows, width, jnp.float32)]
    outs = pl.pallas_call(
        functools.partial(close_kernel, count),
        out_shape=shapes,
        in_specs=[SMEM] + [VMEM] * (4 + count),
        out_specs=[VMEM] * len(shapes),
        scratch_shapes=[
            pltpu.VMEM((count * each, width), jnp.bfloat16),
            pltpu.VMEM((rows, width), jnp.float32),
        ],
        compiler_params=PARAMS,
        name="close",
    )(member.reshape(1), tokens, high, low, begun, *blocks)
    if not whole:
        return outs
    rounded = outs[0].astype(jnp.bfloat16)
    total = outs[0] + tokens.astype(jnp.float32)
    outs = [lax.dynamic_slice_in_dim(total, member * part, part, 1)]
    for k in range(1, inner_count):
        outs.append(lax.dynamic_slice_in_dim(rounded, (member ^ k) * part, part, 1))
    return outs


def final_kernel(*refs):
    out_ref = refs[-1]
    micro, row_count, _ = out_ref.shape
    total = refs[0][...]
    for ref in refs[1:-1]:
        total = total + ref[...].astype(jnp.float32)
    for m in range(micro):
        out_ref[m] = total[m * row_count : (m + 1) * row_count].astype(out_ref.dtype)


def finish(pieces, micro, row_count):
    part = pieces[0].shape[1]
    return pl.pallas_call(
        final_kernel,
        out_shape=jax.ShapeDtypeStruct((micro, row_count, part), jnp.bfloat16),
        in_specs=[VMEM] * len(pieces),
        out_specs=VMEM,
        compiler_params=PARAMS,
        name="finish",
    )(*pieces)


def body(tokens, norm_gain, router, expert_in, expert_out, choices):
    sections = lax.axis_size("section")
    inner_count = lax.axis_size("inner")
    member = lax.axis_index("inner").astype(jnp.int32)
    section = lax.axis_index("section").astype(jnp.int32).reshape(1)
    chips = sections // 2
    experts = router.shape[1]
    per_expert = sections // experts
    micro, row_count, width = tokens.shape
    rows = micro * row_count
    hidden = expert_in.shape[2]
    own = tokens.reshape(rows, width)
    named = choices.transpose(0, 2, 1)
    gain = norm_gain.reshape(1, width)

    other = trade(own, "section", 1)
    other_named = trade(named, "section", 1)
    own, named, gain = fetch((own, named, gain))
    *messages, normed, slots, names = pack(
        section, own, other, named, other_named, gain, chips, per_expert, experts
    )
    order = list(range(1, chips))
    arrived = {k: trade(messages[k], "section", 2 * k) for k in reversed(order)}
    turned_in, router_rows, down = load_weights(
        expert_in[0].reshape(2 * hidden, width), (router.T, expert_out[0]), slots
    )
    far, near = order[-1], order[:-1]
    early = (0, 1, 2 * far, 2 * far + 1)
    late = tuple(distance for k in near for distance in (2 * k, 2 * k + 1))
    high_a, low_a, high_b, low_b = mix(
        section, normed, slots, names, router_rows, early, late, per_expert
    )

    def come_back(blocks, distances):
        return [
            trade(block, "section", distance) if distance else block
            for block, distance in zip(blocks, distances)
        ]

    early_blocks = run_expert([messages[0], arrived[far]], turned_in, down, 2)
    late_blocks = run_expert(
        [arrived[k] for k in near], turned_in, down, 2, (early_blocks[0],)
    )
    begun = begin(high_a, low_a, come_back(early_blocks, early))
    split = close(
        high_b, low_b, begun, come_back(late_blocks, late), own, member, inner_count
    )
    pieces = {k: trade(split[k], "inner", k) for k in reversed(range(1, inner_count))}
    pieces[0] = split[0]
    return finish([pieces[k] for k in [0] + list(reversed(range(1, inner_count)))], micro, row_count)


def solution(mesh):
    return jax.shard_map(
        body,
        mesh=mesh,
        in_specs=(
            P(None, "section", None),
            P(),
            P(),
            P("section", None, "inner", None),
            P("section", "inner", None),
            P(None, "section", None),
        ),
        out_specs=P(None, "section", "inner"),
        check_vma=False,
    )
```

```python
import functools

import jax
import jax.numpy as jnp
from jax import lax
from jax.experimental import pallas as pl
from jax.experimental.pallas import tpu as pltpu
from jax.sharding import PartitionSpec as P

epsilon = 1e-05
LANES = 128
NT = (((1,), (1,)), ((), ()))
VMEM = pl.BlockSpec(memory_space=pltpu.VMEM)
ANY = pl.BlockSpec(memory_space=pl.ANY)
HBM = pl.BlockSpec(memory_space=pltpu.HBM)
SMEM = pl.BlockSpec(memory_space=pltpu.SMEM)
PARAMS = pltpu.CompilerParams(vmem_limit_bytes=20 * 1024 * 1024)


def trade(value, axis, distance):
    count = lax.axis_size(axis)
    return lax.ppermute(value, axis, [(place, place ^ distance) for place in range(count)])


def visit(value, step, cross):
    count = lax.axis_size("section")
    pairs = [(place, place ^ (2 * step[place % 2]) ^ cross) for place in range(count)]
    return lax.ppermute(value, "section", pairs)


def shaped(rows, width, dtype):
    return jax.ShapeDtypeStruct((rows, width), dtype)


def expert_at(section, distances, per_expert):
    distance = jnp.where(section % 2 == 0, distances[0], distances[1])
    return lax.div(section ^ distance, jnp.int32(per_expert)).astype(jnp.float32)


def slots_of(named, experts, row_count):
    rows = named[0].shape[1]
    ids = lax.broadcasted_iota(jnp.int32, (experts, rows), 0).astype(jnp.float32)
    hit = (named[0] == ids) | (named[1] == ids)
    above = lax.broadcasted_iota(jnp.int32, (rows, rows), 0)
    column = lax.broadcasted_iota(jnp.int32, (rows, rows), 1)
    earlier = (above < column) & (above // row_count == column // row_count)
    rank = jnp.dot(
        hit.astype(jnp.bfloat16), earlier.astype(jnp.bfloat16), preferred_element_type=jnp.float32
    )
    group = lax.broadcasted_iota(jnp.int32, (experts, rows), 1) // row_count
    return jnp.where(hit, (group * (row_count // 2)).astype(jnp.float32) + rank, -1.0)


def picked(section, slots, normed, steps, per_expert):
    experts, rows = slots.shape
    ids = lax.broadcasted_iota(jnp.int32, (experts, rows), 0).astype(jnp.float32)
    slot_ids = lax.broadcasted_iota(jnp.int32, (rows // 2, rows), 0).astype(jnp.float32)
    picks = []
    for step in steps:
        expert = expert_at(section, (2 * step[0], 2 * step[1]), per_expert)
        slot = jnp.sum(jnp.where(ids == expert, slots, 0.0), axis=0, keepdims=True)
        picks.append(jnp.where(slot == slot_ids, 1.0, 0.0))
    pick = jnp.concatenate(picks, axis=0).astype(jnp.bfloat16)
    return jnp.dot(pick, normed, preferred_element_type=jnp.float32).astype(jnp.bfloat16)


def normed_of(values, gain):
    values = values.astype(jnp.float32)
    inv_rms = lax.rsqrt(jnp.mean(values * values, axis=-1, keepdims=True) + epsilon)
    return (values * inv_rms * gain).astype(jnp.bfloat16)


def named_of(ref):
    micro = ref.shape[0]
    return [
        jnp.concatenate([ref[m, k : k + 1, :] for m in range(micro)], axis=1).astype(jnp.float32)
        for k in range(2)
    ]


def own_kernel(steps, per_expert, section_ref, tokens_ref, named_ref, gain_ref, *refs):
    half_refs, refs = refs[: len(steps)], refs[len(steps) :]
    own_ref, gain_out_ref, normed_ref, slots_ref, names_ref, held_ref, sems = refs
    copies = [
        pltpu.make_async_copy(source, target, sems.at[k])
        for k, (source, target) in enumerate(
            [(named_ref, held_ref), (gain_ref, gain_out_ref), (tokens_ref, own_ref)]
        )
    ]
    for copy in copies:
        copy.start()
    copies[0].wait()
    named = named_of(held_ref)
    slots = slots_of(named, slots_ref.shape[0], named_ref.shape[2])
    slots_ref[...] = slots
    names_ref[0:1, :] = named[0]
    names_ref[1:2, :] = named[1]
    copies[1].wait()
    copies[2].wait()
    normed = normed_of(own_ref[...], gain_out_ref[...])
    normed_ref[...] = normed
    packed = picked(section_ref[0], slots, normed, steps, per_expert)
    each = packed.shape[0] // len(steps)
    for place, half_ref in enumerate(half_refs):
        half_ref[...] = packed[place * each : (place + 1) * each, :]


def own_part(section, tokens, named, gain, steps, per_expert, experts):
    rows, width = tokens.shape
    arrays = [pltpu.with_memory_space_constraint(a, pltpu.HBM) for a in (tokens, named, gain)]
    shapes = [shaped(rows // 2, width, jnp.bfloat16)] * len(steps) + [
        shaped(rows, width, jnp.bfloat16),
        shaped(1, width, jnp.float32),
        shaped(rows, width, jnp.bfloat16),
        shaped(experts, rows, jnp.float32),
        shaped(2, rows, jnp.float32),
    ]
    return pl.pallas_call(
        functools.partial(own_kernel, steps, per_expert),
        out_shape=shapes,
        in_specs=[SMEM] + [HBM] * 3,
        out_specs=[VMEM] * len(shapes),
        scratch_shapes=[pltpu.VMEM(named.shape, jnp.int32), pltpu.SemaphoreType.DMA((3,))],
        compiler_params=PARAMS,
        name="own_part",
    )(section, *arrays)


def other_kernel(steps, per_expert, section_ref, other_ref, named_ref, gain_ref, *refs):
    count = len(steps)
    half_refs, out_refs, normed_ref, slots_ref = refs[:count], refs[count:-2], refs[-2], refs[-1]
    slots = slots_of(named_of(named_ref), slots_ref.shape[0], named_ref.shape[2])
    slots_ref[...] = slots
    normed = normed_of(other_ref[...], gain_ref[...])
    normed_ref[...] = normed
    packed = picked(section_ref[0], slots, normed, steps, per_expert)
    each = packed.shape[0] // count
    for place, (half_ref, out_ref) in enumerate(zip(half_refs, out_refs)):
        out_ref[:each, :] = half_ref[...]
        out_ref[each:, :] = packed[place * each : (place + 1) * each, :]


def other_part(section, other, named, gain, halves, steps, per_expert, experts):
    rows, width = other.shape
    shapes = [shaped(rows, width, jnp.bfloat16)] * (len(steps) + 1)
    shapes.append(shaped(experts, rows, jnp.float32))
    return pl.pallas_call(
        functools.partial(other_kernel, steps, per_expert),
        out_shape=shapes,
        in_specs=[SMEM] + [VMEM] * (3 + len(halves)),
        out_specs=[VMEM] * len(shapes),
        compiler_params=PARAMS,
        name="other_part",
    )(section, other, named, gain, *halves)


def mix_kernel(sets, per_expert, section_ref, normed_ref, slots_ref, named_ref, router_ref, *outs):
    experts, every = slots_ref.shape
    logits = lax.dot_general(
        normed_ref[...], router_ref[...], NT, preferred_element_type=jnp.float32
    )
    diagonal = lax.broadcasted_iota(jnp.int32, (every, every), 0) == (
        lax.broadcasted_iota(jnp.int32, (every, every), 1)
    )

    def upright(row):
        return jnp.sum(jnp.where(diagonal, row, 0.0), axis=1, keepdims=True)

    first, second = upright(named_ref[0:1, :]), upright(named_ref[1:2, :])
    ids = lax.broadcasted_iota(jnp.int32, logits.shape, 1).astype(jnp.float32)
    lead = jnp.sum(jnp.where(first == ids, logits, 0.0), axis=1, keepdims=True)
    trail = jnp.sum(jnp.where(second == ids, logits, 0.0), axis=1, keepdims=True)
    weight_a = 1.0 / (1.0 + jnp.exp(trail - lead))
    weight_b = 1.0 / (1.0 + jnp.exp(lead - trail))
    section = section_ref[0]
    tall = lax.broadcasted_iota(jnp.int32, (experts, every), 0).astype(jnp.float32)
    for place, distances in enumerate(sets):
        high_ref, low_ref = outs[2 * place : 2 * place + 2]
        count, width = high_ref.shape
        each = width // len(distances)
        lanes = lax.broadcasted_iota(jnp.int32, (count, width), 1).astype(jnp.float32)
        spread = jnp.zeros((count, width), jnp.float32)
        for at, distance in enumerate(distances):
            expert = expert_at(section, distance, per_expert)
            slot = jnp.sum(jnp.where(tall == expert, slots_ref[...], 0.0), axis=0, keepdims=True)
            weight = jnp.where(first == expert, weight_a, 0.0) + jnp.where(
                second == expert, weight_b, 0.0
            )
            spread = spread + jnp.where(
                upright(slot) + at * each == lanes, weight, 0.0
            )
        high = spread.astype(jnp.bfloat16)
        high_ref[...] = high
        low_ref[...] = (spread - high.astype(jnp.float32)).astype(jnp.bfloat16)


def mix(section, normed, slots, named, router, early, near, per_expert):
    rows = normed.shape[0]
    shapes = [
        shaped(rows, len(distances) * rows // 2, jnp.bfloat16)
        for distances in (early, near)
        for _ in range(2)
    ]
    return pl.pallas_call(
        functools.partial(mix_kernel, (early, near), per_expert),
        out_shape=shapes,
        in_specs=[SMEM] + [VMEM] * 4,
        out_specs=[VMEM] * len(shapes),
        compiler_params=PARAMS,
        name="mix",
    )(section, normed, slots, named, router)


def load_kernel(count, steps, per_expert, section_ref, in_ref, *refs):
    sources, refs = refs[:count], refs[count:]
    normed_refs, slots_refs, refs = refs[:2], refs[2:4], refs[4:]
    turned_ref, targets, out_refs = refs[0], refs[1 : 1 + count], refs[1 + count : -2]
    held_ref, sems = refs[-2:]
    pieces, rows, _ = held_ref.shape
    copies = [
        pltpu.make_async_copy(in_ref.at[pl.ds(k * rows, rows)], held_ref.at[k], sems.at[k])
        for k in range(pieces)
    ]
    others = [
        pltpu.make_async_copy(source, target, sems.at[pieces + k])
        for k, (source, target) in enumerate(zip(sources, targets))
    ]
    for copy in copies + others:
        copy.start()
    for part, (normed_ref, slots_ref) in enumerate(zip(normed_refs, slots_refs)):
        packed = picked(section_ref[0], slots_ref[...], normed_ref[...], steps, per_expert)
        each = packed.shape[0] // len(steps)
        for place, out_ref in enumerate(out_refs):
            out_ref[part * each : (part + 1) * each, :] = packed[
                place * each : (place + 1) * each, :
            ]
    for k in range(pieces):
        copies[k].wait()
        turned_ref[:, k * rows : (k + 1) * rows] = held_ref[k].T
    for copy in others:
        copy.wait()


def load_weights(section, stacked_in, others, normed, slots, steps, per_expert):
    count = len(others)
    rows, width = stacked_in.shape
    pieces = max(1, rows // LANES)
    arrays = [pltpu.with_memory_space_constraint(a, pltpu.HBM) for a in (stacked_in, *others)]
    shapes = [shaped(width, rows, stacked_in.dtype)]
    shapes += [jax.ShapeDtypeStruct(a.shape, a.dtype) for a in others]
    shapes += [shaped(normed[0].shape[0], width, jnp.bfloat16)] * len(steps)
    return pl.pallas_call(
        functools.partial(load_kernel, count, steps, per_expert),
        out_shape=shapes,
        in_specs=[SMEM] + [HBM] * (count + 1) + [VMEM] * 4,
        out_specs=[VMEM] * len(shapes),
        scratch_shapes=[
            pltpu.VMEM((pieces, rows // pieces, width), stacked_in.dtype),
            pltpu.SemaphoreType.DMA((pieces + count,)),
        ],
        compiler_params=PARAMS,
        name="load_weights",
    )(section, *arrays, *normed, *slots)


def expert_kernel(count, after, in_ref, down_ref, *refs):
    blocks, every_ref = refs[:count], refs[-1]
    out_refs = refs[count + after : -1]
    every = gathered(blocks, every_ref)
    gate_up = jnp.dot(every, in_ref[...], preferred_element_type=jnp.float32)
    hidden = gate_up.shape[1] // 2
    gate = gate_up[:, :hidden]
    active = (gate / (1.0 + jnp.exp(-gate)) * gate_up[:, hidden:]).astype(jnp.bfloat16)
    partial = jnp.dot(active, down_ref[...], preferred_element_type=jnp.float32)
    rows = out_refs[0].shape[0]
    for place, out_ref in enumerate(out_refs):
        out_ref[...] = partial[place * rows : (place + 1) * rows, :].astype(jnp.bfloat16)


def run_expert(blocks, turned_in, down, pieces, after=()):
    count = len(blocks)
    rows, width = blocks[0].shape
    return pl.pallas_call(
        functools.partial(expert_kernel, count, len(after)),
        out_shape=[shaped(rows // pieces, width, jnp.bfloat16)] * (count * pieces),
        in_specs=[VMEM] * (2 + count) + [ANY] * len(after),
        out_specs=[VMEM] * (count * pieces),
        scratch_shapes=[pltpu.VMEM((count * rows, width), jnp.bfloat16)],
        compiler_params=PARAMS,
        name="expert",
    )(turned_in, down, *blocks, *after)


def gathered(blocks, every_ref):
    rows = blocks[0].shape[0]
    for place, block in enumerate(blocks):
        every_ref[place * rows : (place + 1) * rows, :] = block[...]
    return every_ref[...]


def begin_kernel(count, high_ref, low_ref, *refs):
    blocks, out_ref, every_ref = refs[:count], refs[count], refs[-1]
    every = gathered(blocks, every_ref)
    total = jnp.dot(low_ref[...], every, preferred_element_type=jnp.float32)
    out_ref[...] = total + jnp.dot(high_ref[...], every, preferred_element_type=jnp.float32)


def begin(high, low, blocks):
    count = len(blocks)
    each, width = blocks[0].shape
    return pl.pallas_call(
        functools.partial(begin_kernel, count),
        out_shape=shaped(high.shape[0], width, jnp.float32),
        in_specs=[VMEM] * (2 + count),
        out_specs=VMEM,
        scratch_shapes=[pltpu.VMEM((count * each, width), jnp.bfloat16)],
        compiler_params=PARAMS,
        name="begin",
    )(high, low, *blocks)


def close_kernel(count, member_ref, tokens_ref, high_ref, low_ref, begun_ref, *refs):
    blocks, outs, every_ref, total_ref = refs[:count], refs[count:-2], refs[-2], refs[-1]
    every = gathered(blocks, every_ref)
    total = begun_ref[...] + jnp.dot(low_ref[...], every, preferred_element_type=jnp.float32)
    total_ref[...] = total + jnp.dot(high_ref[...], every, preferred_element_type=jnp.float32)
    if len(outs) == 1:
        outs[0][...] = total_ref[...]
        return
    part = outs[0].shape[1]
    for k, out_ref in enumerate(outs):
        columns = pl.ds(pl.multiple_of((member_ref[0] ^ k) * part, LANES), part)
        value = total_ref[:, columns]
        if k == 0:
            value = value + tokens_ref[:, columns].astype(jnp.float32)
        out_ref[...] = value.astype(out_ref.dtype)


def close(high, low, begun, blocks, tokens, member, inner_count):
    count = len(blocks)
    each = blocks[0].shape[0]
    rows, width = begun.shape
    part = width // inner_count
    whole = part % LANES != 0
    kinds = [jnp.float32] + [jnp.bfloat16] * (inner_count - 1)
    shapes = [shaped(rows, part, kind) for kind in kinds]
    if whole:
        shapes = [shaped(rows, width, jnp.float32)]
    outs = pl.pallas_call(
        functools.partial(close_kernel, count),
        out_shape=shapes,
        in_specs=[SMEM] + [VMEM] * (4 + count),
        out_specs=[VMEM] * len(shapes),
        scratch_shapes=[
            pltpu.VMEM((count * each, width), jnp.bfloat16),
            pltpu.VMEM((rows, width), jnp.float32),
        ],
        compiler_params=PARAMS,
        name="close",
    )(member.reshape(1), tokens, high, low, begun, *blocks)
    if not whole:
        return outs
    rounded = outs[0].astype(jnp.bfloat16)
    total = outs[0] + tokens.astype(jnp.float32)
    outs = [lax.dynamic_slice_in_dim(total, member * part, part, 1)]
    for k in range(1, inner_count):
        outs.append(lax.dynamic_slice_in_dim(rounded, (member ^ k) * part, part, 1))
    return outs


def final_kernel(*refs):
    out_ref = refs[-1]
    micro, row_count, _ = out_ref.shape
    total = refs[0][...]
    for ref in refs[1:-1]:
        total = total + ref[...].astype(jnp.float32)
    for m in range(micro):
        out_ref[m] = total[m * row_count : (m + 1) * row_count].astype(out_ref.dtype)


def finish(pieces, micro, row_count):
    part = pieces[0].shape[1]
    return pl.pallas_call(
        final_kernel,
        out_shape=jax.ShapeDtypeStruct((micro, row_count, part), jnp.bfloat16),
        in_specs=[VMEM] * len(pieces),
        out_specs=VMEM,
        compiler_params=PARAMS,
        name="finish",
    )(*pieces)


def body(tokens, norm_gain, router, expert_in, expert_out, choices):
    sections = lax.axis_size("section")
    inner_count = lax.axis_size("inner")
    member = lax.axis_index("inner").astype(jnp.int32)
    section = lax.axis_index("section").astype(jnp.int32).reshape(1)
    chips = sections // 2
    experts = router.shape[1]
    per_expert = sections // experts
    micro, row_count, width = tokens.shape
    rows = micro * row_count
    hidden = expert_in.shape[2]
    own = tokens.reshape(rows, width)
    named = choices.transpose(0, 2, 1)
    gain = norm_gain.reshape(1, width)

    far = chips - 1
    first_steps = ((0, 0), (far, far))
    steps = []
    for k in range(1, far, 2):
        steps += [(k, k + 1), (k + 1, k)]

    other = trade(own, "section", 1)
    other_named = trade(named, "section", 1)
    *halves, own, gain, normed, slots, names = own_part(
        section, own, named, gain, first_steps, per_expert, experts
    )
    message, away, other_normed, other_slots = other_part(
        section, other, other_named, gain, halves, first_steps, per_expert, experts
    )
    away = visit(away, (far, far), 0)
    turned_in, router_rows, down, *messages = load_weights(
        section,
        expert_in[0].reshape(2 * hidden, width),
        (router.T, expert_out[0]),
        (normed, other_normed),
        (slots, other_slots),
        tuple(steps),
        per_expert,
    )
    arrived = [visit(value, step, 0) for value, step in zip(messages, steps)]

    def origins(step):
        a, b = step
        return ((2 * a, 2 * b), (2 * b + 1, 2 * a + 1))

    early = origins((0, 0)) + origins((far, far))
    late = tuple(pair for step in steps for pair in origins(step))
    high_a, low_a, high_b, low_b = mix(
        section, normed, slots, names, router_rows, early, late, per_expert
    )
    here, beside, *away = run_expert([message, away], turned_in, down, 2)
    results = run_expert(arrived, turned_in, down, 2, (here,))
    away = [visit(value, (far, far), cross) for cross, value in enumerate(away)]
    begun = begin(high_a, low_a, [here, trade(beside, "section", 1), *away])
    results = [visit(value, steps[j // 2], j % 2) for j, value in enumerate(results)]
    split = close(high_b, low_b, begun, results, own, member, inner_count)
    pieces = {k: trade(split[k], "inner", k) for k in reversed(range(1, inner_count))}
    pieces[0] = split[0]
    return finish([pieces[k] for k in [0] + list(reversed(range(1, inner_count)))], micro, row_count)


def solution(mesh):
    return jax.shard_map(
        body,
        mesh=mesh,
        in_specs=(
            P(None, "section", None),
            P(),
            P(),
            P("section", None, "inner", None),
            P("section", "inner", None),
            P(None, "section", None),
        ),
        out_specs=P(None, "section", "inner"),
        check_vma=False,
    )
```

```python
import functools

import jax
import jax.numpy as jnp
from jax import lax
from jax.experimental import pallas as pl
from jax.experimental.pallas import tpu as pltpu
from jax.sharding import PartitionSpec as P

epsilon = 1e-05
LANES = 128
TOKEN_COPIES = 4
NT = (((1,), (1,)), ((), ()))
VMEM = pl.BlockSpec(memory_space=pltpu.VMEM)
ANY = pl.BlockSpec(memory_space=pl.ANY)
HBM = pl.BlockSpec(memory_space=pltpu.HBM)
SMEM = pl.BlockSpec(memory_space=pltpu.SMEM)
PARAMS = pltpu.CompilerParams(vmem_limit_bytes=20 * 1024 * 1024)


def trade(value, axis, distance):
    count = lax.axis_size(axis)
    return lax.ppermute(value, axis, [(place, place ^ distance) for place in range(count)])


def turn(value, distance):
    count = lax.axis_size("inner")
    pairs = [(place, (place + distance) % count) for place in range(count)]
    return lax.ppermute(value, "inner", pairs)


def visit(value, step, cross):
    count = lax.axis_size("section")
    pairs = [(place, place ^ (2 * step[place % 2]) ^ cross) for place in range(count)]
    return lax.ppermute(value, "section", pairs)


def shaped(rows, width, dtype):
    return jax.ShapeDtypeStruct((rows, width), dtype)


def expert_at(section, distances, per_expert):
    distance = jnp.where(section % 2 == 0, distances[0], distances[1])
    return lax.div(section ^ distance, jnp.int32(per_expert)).astype(jnp.float32)


def slots_of(named, experts, row_count):
    rows = named[0].shape[1]
    ids = lax.broadcasted_iota(jnp.int32, (experts, rows), 0).astype(jnp.float32)
    hit = (named[0] == ids) | (named[1] == ids)
    above = lax.broadcasted_iota(jnp.int32, (rows, rows), 0)
    column = lax.broadcasted_iota(jnp.int32, (rows, rows), 1)
    earlier = (above < column) & (above // row_count == column // row_count)
    rank = jnp.dot(
        hit.astype(jnp.bfloat16), earlier.astype(jnp.bfloat16), preferred_element_type=jnp.float32
    )
    group = lax.broadcasted_iota(jnp.int32, (experts, rows), 1) // row_count
    return jnp.where(hit, (group * (row_count // 2)).astype(jnp.float32) + rank, -1.0)


def picked(section, slots, normed, steps, per_expert):
    experts, rows = slots.shape
    ids = lax.broadcasted_iota(jnp.int32, (experts, rows), 0).astype(jnp.float32)
    slot_ids = lax.broadcasted_iota(jnp.int32, (rows // 2, rows), 0).astype(jnp.float32)
    picks = []
    for step in steps:
        expert = expert_at(section, (2 * step[0], 2 * step[1]), per_expert)
        slot = jnp.sum(jnp.where(ids == expert, slots, 0.0), axis=0, keepdims=True)
        picks.append(jnp.where(slot == slot_ids, 1.0, 0.0))
    pick = jnp.concatenate(picks, axis=0).astype(jnp.bfloat16)
    return jnp.dot(pick, normed, preferred_element_type=jnp.float32).astype(jnp.bfloat16)


def normed_of(values, gain):
    values = values.astype(jnp.float32)
    inv_rms = lax.rsqrt(jnp.mean(values * values, axis=-1, keepdims=True) + epsilon)
    return (values * inv_rms * gain).astype(jnp.bfloat16)


def named_of(ref):
    micro = ref.shape[0]
    return [
        jnp.concatenate([ref[m, k : k + 1, :] for m in range(micro)], axis=1).astype(jnp.float32)
        for k in range(2)
    ]


def own_kernel(steps, per_expert, section_ref, tokens_ref, named_ref, gain_ref, *refs):
    half_refs, refs = refs[: len(steps)], refs[len(steps) :]
    own_ref, gain_out_ref, normed_ref, slots_ref, names_ref, held_ref, sems = refs
    width = tokens_ref.shape[1]
    chunk = width // TOKEN_COPIES
    spans = [pl.ds(k * chunk, chunk) for k in range(TOKEN_COPIES)]
    pairs = [(tokens_ref.at[:, span], own_ref.at[:, span]) for span in spans]
    pairs = [(named_ref, held_ref), *pairs, (gain_ref, gain_out_ref)]
    copies = [
        pltpu.make_async_copy(source, target, sems.at[k])
        for k, (source, target) in enumerate(pairs)
    ]
    for copy in copies:
        copy.start()
    copies[0].wait()
    named = named_of(held_ref)
    slots = slots_of(named, slots_ref.shape[0], named_ref.shape[2])
    slots_ref[...] = slots
    names_ref[0:1, :] = named[0]
    names_ref[1:2, :] = named[1]
    for copy in copies[1:]:
        copy.wait()
    normed = normed_of(own_ref[...], gain_out_ref[...])
    normed_ref[...] = normed
    packed = picked(section_ref[0], slots, normed, steps, per_expert)
    each = packed.shape[0] // len(steps)
    for place, half_ref in enumerate(half_refs):
        half_ref[...] = packed[place * each : (place + 1) * each, :]


def own_part(section, tokens, named, gain, steps, per_expert, experts):
    rows, width = tokens.shape
    arrays = [pltpu.with_memory_space_constraint(a, pltpu.HBM) for a in (tokens, named, gain)]
    shapes = [shaped(rows // 2, width, jnp.bfloat16)] * len(steps) + [
        shaped(rows, width, jnp.bfloat16),
        shaped(1, width, jnp.float32),
        shaped(rows, width, jnp.bfloat16),
        shaped(experts, rows, jnp.float32),
        shaped(2, rows, jnp.float32),
    ]
    return pl.pallas_call(
        functools.partial(own_kernel, steps, per_expert),
        out_shape=shapes,
        in_specs=[SMEM] + [HBM] * 3,
        out_specs=[VMEM] * len(shapes),
        scratch_shapes=[pltpu.VMEM(named.shape, jnp.int32), pltpu.SemaphoreType.DMA((TOKEN_COPIES + 2,))],
        compiler_params=PARAMS,
        name="own_part",
    )(section, *arrays)


def other_kernel(steps, per_expert, section_ref, other_ref, named_ref, gain_ref, *refs):
    count = len(steps)
    half_refs, out_refs, normed_ref, slots_ref = refs[:count], refs[count:-2], refs[-2], refs[-1]
    slots = slots_of(named_of(named_ref), slots_ref.shape[0], named_ref.shape[2])
    slots_ref[...] = slots
    normed = normed_of(other_ref[...], gain_ref[...])
    normed_ref[...] = normed
    packed = picked(section_ref[0], slots, normed, steps, per_expert)
    each = packed.shape[0] // count
    for place, (half_ref, out_ref) in enumerate(zip(half_refs, out_refs)):
        out_ref[:each, :] = half_ref[...]
        out_ref[each:, :] = packed[place * each : (place + 1) * each, :]


def other_part(section, other, named, gain, halves, steps, per_expert, experts):
    rows, width = other.shape
    shapes = [shaped(rows, width, jnp.bfloat16)] * (len(steps) + 1)
    shapes.append(shaped(experts, rows, jnp.float32))
    return pl.pallas_call(
        functools.partial(other_kernel, steps, per_expert),
        out_shape=shapes,
        in_specs=[SMEM] + [VMEM] * (3 + len(halves)),
        out_specs=[VMEM] * len(shapes),
        compiler_params=PARAMS,
        name="other_part",
    )(section, other, named, gain, *halves)


def mix_kernel(sets, per_expert, section_ref, normed_ref, slots_ref, named_ref, router_ref, *outs):
    experts, every = slots_ref.shape
    logits = lax.dot_general(
        normed_ref[...], router_ref[...], NT, preferred_element_type=jnp.float32
    )
    diagonal = lax.broadcasted_iota(jnp.int32, (every, every), 0) == (
        lax.broadcasted_iota(jnp.int32, (every, every), 1)
    )

    def upright(row):
        return jnp.sum(jnp.where(diagonal, row, 0.0), axis=1, keepdims=True)

    first, second = upright(named_ref[0:1, :]), upright(named_ref[1:2, :])
    ids = lax.broadcasted_iota(jnp.int32, logits.shape, 1).astype(jnp.float32)
    lead = jnp.sum(jnp.where(first == ids, logits, 0.0), axis=1, keepdims=True)
    trail = jnp.sum(jnp.where(second == ids, logits, 0.0), axis=1, keepdims=True)
    weight_a = 1.0 / (1.0 + jnp.exp(trail - lead))
    weight_b = 1.0 / (1.0 + jnp.exp(lead - trail))
    section = section_ref[0]
    tall = lax.broadcasted_iota(jnp.int32, (experts, every), 0).astype(jnp.float32)
    for place, distances in enumerate(sets):
        high_ref, low_ref = outs[2 * place : 2 * place + 2]
        count, width = high_ref.shape
        each = width // len(distances)
        lanes = lax.broadcasted_iota(jnp.int32, (count, width), 1).astype(jnp.float32)
        spread = jnp.zeros((count, width), jnp.float32)
        for at, distance in enumerate(distances):
            expert = expert_at(section, distance, per_expert)
            slot = jnp.sum(jnp.where(tall == expert, slots_ref[...], 0.0), axis=0, keepdims=True)
            weight = jnp.where(first == expert, weight_a, 0.0) + jnp.where(
                second == expert, weight_b, 0.0
            )
            spread = spread + jnp.where(
                upright(slot) + at * each == lanes, weight, 0.0
            )
        high = spread.astype(jnp.bfloat16)
        high_ref[...] = high
        low_ref[...] = (spread - high.astype(jnp.float32)).astype(jnp.bfloat16)


def mix(section, normed, slots, named, router, early, near, per_expert):
    rows = normed.shape[0]
    shapes = [
        shaped(rows, len(distances) * rows // 2, jnp.bfloat16)
        for distances in (early, near)
        for _ in range(2)
    ]
    return pl.pallas_call(
        functools.partial(mix_kernel, (early, near), per_expert),
        out_shape=shapes,
        in_specs=[SMEM] + [VMEM] * 4,
        out_specs=[VMEM] * len(shapes),
        compiler_params=PARAMS,
        name="mix",
    )(section, normed, slots, named, router)


def load_kernel(count, steps, per_expert, section_ref, in_ref, *refs):
    sources, refs = refs[:count], refs[count:]
    normed_refs, slots_refs, refs = refs[:2], refs[2:4], refs[4:]
    turned_ref, targets, out_refs = refs[0], refs[1 : 1 + count], refs[1 + count : -2]
    held_ref, sems = refs[-2:]
    pieces, rows, _ = held_ref.shape
    copies = [
        pltpu.make_async_copy(in_ref.at[pl.ds(k * rows, rows)], held_ref.at[k], sems.at[k])
        for k in range(pieces)
    ]
    others = [
        pltpu.make_async_copy(source, target, sems.at[pieces + k])
        for k, (source, target) in enumerate(zip(sources, targets))
    ]
    for copy in copies + others:
        copy.start()
    for part, (normed_ref, slots_ref) in enumerate(zip(normed_refs, slots_refs)):
        packed = picked(section_ref[0], slots_ref[...], normed_ref[...], steps, per_expert)
        each = packed.shape[0] // len(steps)
        for place, out_ref in enumerate(out_refs):
            out_ref[part * each : (part + 1) * each, :] = packed[
                place * each : (place + 1) * each, :
            ]
    for k in range(pieces):
        copies[k].wait()
        turned_ref[:, k * rows : (k + 1) * rows] = held_ref[k].T
    for copy in others:
        copy.wait()


def load_weights(section, stacked_in, others, normed, slots, steps, per_expert):
    count = len(others)
    rows, width = stacked_in.shape
    pieces = max(1, rows // LANES)
    arrays = [pltpu.with_memory_space_constraint(a, pltpu.HBM) for a in (stacked_in, *others)]
    shapes = [shaped(width, rows, stacked_in.dtype)]
    shapes += [jax.ShapeDtypeStruct(a.shape, a.dtype) for a in others]
    shapes += [shaped(normed[0].shape[0], width, jnp.bfloat16)] * len(steps)
    return pl.pallas_call(
        functools.partial(load_kernel, count, steps, per_expert),
        out_shape=shapes,
        in_specs=[SMEM] + [HBM] * (count + 1) + [VMEM] * 4,
        out_specs=[VMEM] * len(shapes),
        scratch_shapes=[
            pltpu.VMEM((pieces, rows // pieces, width), stacked_in.dtype),
            pltpu.SemaphoreType.DMA((pieces + count,)),
        ],
        compiler_params=PARAMS,
        name="load_weights",
    )(section, *arrays, *normed, *slots)


def expert_kernel(count, after, in_ref, down_ref, *refs):
    blocks, every_ref = refs[:count], refs[-1]
    out_refs = refs[count + after : -1]
    every = gathered(blocks, every_ref)
    gate_up = jnp.dot(every, in_ref[...], preferred_element_type=jnp.float32)
    hidden = gate_up.shape[1] // 2
    gate = gate_up[:, :hidden]
    active = (gate / (1.0 + jnp.exp(-gate)) * gate_up[:, hidden:]).astype(jnp.bfloat16)
    partial = jnp.dot(active, down_ref[...], preferred_element_type=jnp.float32)
    rows = out_refs[0].shape[0]
    for place, out_ref in enumerate(out_refs):
        out_ref[...] = partial[place * rows : (place + 1) * rows, :].astype(jnp.bfloat16)


def run_expert(blocks, turned_in, down, pieces, after=()):
    count = len(blocks)
    rows, width = blocks[0].shape
    return pl.pallas_call(
        functools.partial(expert_kernel, count, len(after)),
        out_shape=[shaped(rows // pieces, width, jnp.bfloat16)] * (count * pieces),
        in_specs=[VMEM] * (2 + count) + [ANY] * len(after),
        out_specs=[VMEM] * (count * pieces),
        scratch_shapes=[pltpu.VMEM((count * rows, width), jnp.bfloat16)],
        compiler_params=PARAMS,
        name="expert",
    )(turned_in, down, *blocks, *after)


def gathered(blocks, every_ref):
    rows = blocks[0].shape[0]
    for place, block in enumerate(blocks):
        every_ref[place * rows : (place + 1) * rows, :] = block[...]
    return every_ref[...]


def begin_kernel(count, high_ref, low_ref, *refs):
    blocks, out_ref, every_ref = refs[:count], refs[count], refs[-1]
    every = gathered(blocks, every_ref)
    total = jnp.dot(low_ref[...], every, preferred_element_type=jnp.float32)
    out_ref[...] = total + jnp.dot(high_ref[...], every, preferred_element_type=jnp.float32)


def begin(high, low, blocks):
    count = len(blocks)
    each, width = blocks[0].shape
    return pl.pallas_call(
        functools.partial(begin_kernel, count),
        out_shape=shaped(high.shape[0], width, jnp.float32),
        in_specs=[VMEM] * (2 + count),
        out_specs=VMEM,
        scratch_shapes=[pltpu.VMEM((count * each, width), jnp.bfloat16)],
        compiler_params=PARAMS,
        name="begin",
    )(high, low, *blocks)


def close_kernel(count, member_ref, tokens_ref, high_ref, low_ref, begun_ref, *refs):
    blocks, outs, every_ref, total_ref = refs[:count], refs[count:-2], refs[-2], refs[-1]
    every = gathered(blocks, every_ref)
    total = begun_ref[...] + jnp.dot(low_ref[...], every, preferred_element_type=jnp.float32)
    total_ref[...] = total + jnp.dot(high_ref[...], every, preferred_element_type=jnp.float32)
    if len(outs) == 1:
        outs[0][...] = total_ref[...]
        return
    part = outs[0].shape[1]
    for k, out_ref in enumerate(outs):
        columns = pl.ds(pl.multiple_of(lax.rem(member_ref[0] + k, len(outs)) * part, LANES), part)
        value = total_ref[:, columns]
        if k == 0:
            value = value + tokens_ref[:, columns].astype(jnp.float32)
        out_ref[...] = value.astype(out_ref.dtype)


def close(high, low, begun, blocks, tokens, member, inner_count):
    count = len(blocks)
    each = blocks[0].shape[0]
    rows, width = begun.shape
    part = width // inner_count
    whole = part % LANES != 0
    kinds = [jnp.float32] + [jnp.bfloat16] * (inner_count - 1)
    shapes = [shaped(rows, part, kind) for kind in kinds]
    if whole:
        shapes = [shaped(rows, width, jnp.float32)]
    outs = pl.pallas_call(
        functools.partial(close_kernel, count),
        out_shape=shapes,
        in_specs=[SMEM] + [VMEM] * (4 + count),
        out_specs=[VMEM] * len(shapes),
        scratch_shapes=[
            pltpu.VMEM((count * each, width), jnp.bfloat16),
            pltpu.VMEM((rows, width), jnp.float32),
        ],
        compiler_params=PARAMS,
        name="close",
    )(member.reshape(1), tokens, high, low, begun, *blocks)
    if not whole:
        return outs
    rounded = outs[0].astype(jnp.bfloat16)
    total = outs[0] + tokens.astype(jnp.float32)
    outs = [lax.dynamic_slice_in_dim(total, member * part, part, 1)]
    for k in range(1, inner_count):
        place = lax.rem(member + k, inner_count)
        outs.append(lax.dynamic_slice_in_dim(rounded, place * part, part, 1))
    return outs


def final_kernel(*refs):
    out_ref = refs[-1]
    micro, row_count, _ = out_ref.shape
    total = refs[0][...]
    for ref in refs[1:-1]:
        total = total + ref[...].astype(jnp.float32)
    for m in range(micro):
        out_ref[m] = total[m * row_count : (m + 1) * row_count].astype(out_ref.dtype)


def finish(pieces, micro, row_count):
    part = pieces[0].shape[1]
    return pl.pallas_call(
        final_kernel,
        out_shape=jax.ShapeDtypeStruct((micro, row_count, part), jnp.bfloat16),
        in_specs=[VMEM] * len(pieces),
        out_specs=VMEM,
        compiler_params=PARAMS,
        name="finish",
    )(*pieces)


def body(tokens, norm_gain, router, expert_in, expert_out, choices):
    sections = lax.axis_size("section")
    inner_count = lax.axis_size("inner")
    member = lax.axis_index("inner").astype(jnp.int32)
    section = lax.axis_index("section").astype(jnp.int32).reshape(1)
    chips = sections // 2
    experts = router.shape[1]
    per_expert = sections // experts
    micro, row_count, width = tokens.shape
    rows = micro * row_count
    hidden = expert_in.shape[2]
    own = tokens.reshape(rows, width)
    named = choices.transpose(0, 2, 1)
    gain = norm_gain.reshape(1, width)

    far = chips - 1
    first_steps = ((0, 0), (far, far))
    steps = []
    for k in range(1, far, 2):
        steps += [(k, k + 1), (k + 1, k)]

    other = trade(own, "section", 1)
    other_named = trade(named, "section", 1)
    *halves, own, gain, normed, slots, names = own_part(
        section, own, named, gain, first_steps, per_expert, experts
    )
    message, away, other_normed, other_slots = other_part(
        section, other, other_named, gain, halves, first_steps, per_expert, experts
    )
    away = visit(away, (far, far), 0)
    turned_in, router_rows, down, *messages = load_weights(
        section,
        expert_in[0].reshape(2 * hidden, width),
        (router.T, expert_out[0]),
        (normed, other_normed),
        (slots, other_slots),
        tuple(steps),
        per_expert,
    )
    arrived = [visit(value, step, 0) for value, step in zip(messages, steps)]

    def origins(step):
        a, b = step
        return ((2 * a, 2 * b), (2 * b + 1, 2 * a + 1))

    early = origins((far, far)) + origins((0, 0))
    late = tuple(pair for step in steps for pair in origins(step))
    high_a, low_a, high_b, low_b = mix(
        section, normed, slots, names, router_rows, early, late, per_expert
    )
    here, beside, *away = run_expert([message, away], turned_in, down, 2)
    results = run_expert(arrived, turned_in, down, 2, (here,))
    away = [visit(value, (far, far), cross) for cross, value in enumerate(away)]
    begun = begin(high_a, low_a, [*away, here, trade(beside, "section", 1)])
    results = [visit(value, steps[j // 2], j % 2) for j, value in enumerate(results)]
    split = close(high_b, low_b, begun, results, own, member, inner_count)
    pieces = {k: turn(split[k], k) for k in range(1, inner_count)}
    pieces[0] = split[0]
    return finish([pieces[k] for k in range(inner_count)], micro, row_count)


def solution(mesh):
    return jax.shard_map(
        body,
        mesh=mesh,
        in_specs=(
            P(None, "section", None),
            P(),
            P(),
            P("section", None, "inner", None),
            P("section", "inner", None),
            P(None, "section", None),
        ),
        out_specs=P(None, "section", "inner"),
        check_vma=False,
    )
```

```python
import functools

import jax
import jax.numpy as jnp
from jax import lax
from jax.experimental import pallas as pl
from jax.experimental.pallas import tpu as pltpu
from jax.sharding import PartitionSpec as P

epsilon = 1e-05
LANES = 128
INNER_ORDER = ((1, 2, 3, 0), (2, 3, 0, 1), (3, 0, 1, 2))
TOKEN_COPIES = 4
NT = (((1,), (1,)), ((), ()))
VMEM = pl.BlockSpec(memory_space=pltpu.VMEM)
ANY = pl.BlockSpec(memory_space=pl.ANY)
HBM = pl.BlockSpec(memory_space=pltpu.HBM)
SMEM = pl.BlockSpec(memory_space=pltpu.SMEM)
PARAMS = pltpu.CompilerParams(vmem_limit_bytes=20 * 1024 * 1024)


def trade(value, axis, distance):
    count = lax.axis_size(axis)
    return lax.ppermute(value, axis, [(place, place ^ distance) for place in range(count)])


def inner_targets(count):
    if count == len(INNER_ORDER[0]):
        return INNER_ORDER
    return tuple(
        tuple((place + k) % count for place in range(count)) for k in range(1, count)
    )


def target_of(member, targets):
    return sum(jnp.where(member == place, target, 0) for place, target in enumerate(targets))


def turn(value, targets):
    return lax.ppermute(value, "inner", list(enumerate(targets)))


def visit(value, step, cross):
    count = lax.axis_size("section")
    pairs = [(place, place ^ (2 * step[place % 2]) ^ cross) for place in range(count)]
    return lax.ppermute(value, "section", pairs)


def shaped(rows, width, dtype):
    return jax.ShapeDtypeStruct((rows, width), dtype)


def expert_at(section, distances, per_expert):
    distance = jnp.where(section % 2 == 0, distances[0], distances[1])
    return lax.div(section ^ distance, jnp.int32(per_expert)).astype(jnp.float32)


def slots_of(named, experts, row_count):
    rows = named[0].shape[1]
    ids = lax.broadcasted_iota(jnp.int32, (experts, rows), 0).astype(jnp.float32)
    hit = (named[0] == ids) | (named[1] == ids)
    above = lax.broadcasted_iota(jnp.int32, (rows, rows), 0)
    column = lax.broadcasted_iota(jnp.int32, (rows, rows), 1)
    earlier = (above < column) & (above // row_count == column // row_count)
    rank = jnp.dot(
        hit.astype(jnp.bfloat16), earlier.astype(jnp.bfloat16), preferred_element_type=jnp.float32
    )
    group = lax.broadcasted_iota(jnp.int32, (experts, rows), 1) // row_count
    return jnp.where(hit, (group * (row_count // 2)).astype(jnp.float32) + rank, -1.0)


def picked(section, slots, normed, steps, per_expert):
    experts, rows = slots.shape
    ids = lax.broadcasted_iota(jnp.int32, (experts, rows), 0).astype(jnp.float32)
    slot_ids = lax.broadcasted_iota(jnp.int32, (rows // 2, rows), 0).astype(jnp.float32)
    picks = []
    for step in steps:
        expert = expert_at(section, (2 * step[0], 2 * step[1]), per_expert)
        slot = jnp.sum(jnp.where(ids == expert, slots, 0.0), axis=0, keepdims=True)
        picks.append(jnp.where(slot == slot_ids, 1.0, 0.0))
    pick = jnp.concatenate(picks, axis=0).astype(jnp.bfloat16)
    return jnp.dot(pick, normed, preferred_element_type=jnp.float32).astype(jnp.bfloat16)


def normed_of(values, gain):
    values = values.astype(jnp.float32)
    inv_rms = lax.rsqrt(jnp.mean(values * values, axis=-1, keepdims=True) + epsilon)
    return (values * inv_rms * gain).astype(jnp.bfloat16)


def named_of(ref):
    micro = ref.shape[0]
    return [
        jnp.concatenate([ref[m, k : k + 1, :] for m in range(micro)], axis=1).astype(jnp.float32)
        for k in range(2)
    ]


def own_kernel(steps, per_expert, section_ref, tokens_ref, named_ref, gain_ref, *refs):
    half_refs, refs = refs[: len(steps)], refs[len(steps) :]
    own_ref, gain_out_ref, normed_ref, slots_ref, names_ref, held_ref, sems = refs
    width = tokens_ref.shape[1]
    chunk = width // TOKEN_COPIES
    spans = [pl.ds(k * chunk, chunk) for k in range(TOKEN_COPIES)]
    pairs = [(tokens_ref.at[:, span], own_ref.at[:, span]) for span in spans]
    pairs = [(named_ref, held_ref), *pairs, (gain_ref, gain_out_ref)]
    copies = [
        pltpu.make_async_copy(source, target, sems.at[k])
        for k, (source, target) in enumerate(pairs)
    ]
    for copy in copies:
        copy.start()
    copies[0].wait()
    named = named_of(held_ref)
    slots = slots_of(named, slots_ref.shape[0], named_ref.shape[2])
    slots_ref[...] = slots
    names_ref[0:1, :] = named[0]
    names_ref[1:2, :] = named[1]
    for copy in copies[1:]:
        copy.wait()
    normed = normed_of(own_ref[...], gain_out_ref[...])
    normed_ref[...] = normed
    packed = picked(section_ref[0], slots, normed, steps, per_expert)
    each = packed.shape[0] // len(steps)
    for place, half_ref in enumerate(half_refs):
        half_ref[...] = packed[place * each : (place + 1) * each, :]


def own_part(section, tokens, named, gain, steps, per_expert, experts):
    rows, width = tokens.shape
    arrays = [pltpu.with_memory_space_constraint(a, pltpu.HBM) for a in (tokens, named, gain)]
    shapes = [shaped(rows // 2, width, jnp.bfloat16)] * len(steps) + [
        shaped(rows, width, jnp.bfloat16),
        shaped(1, width, jnp.float32),
        shaped(rows, width, jnp.bfloat16),
        shaped(experts, rows, jnp.float32),
        shaped(2, rows, jnp.float32),
    ]
    return pl.pallas_call(
        functools.partial(own_kernel, steps, per_expert),
        out_shape=shapes,
        in_specs=[SMEM] + [HBM] * 3,
        out_specs=[VMEM] * len(shapes),
        scratch_shapes=[pltpu.VMEM(named.shape, jnp.int32), pltpu.SemaphoreType.DMA((TOKEN_COPIES + 2,))],
        compiler_params=PARAMS,
        name="own_part",
    )(section, *arrays)


def other_kernel(steps, per_expert, section_ref, other_ref, named_ref, gain_ref, *refs):
    count = len(steps)
    half_refs, out_refs, normed_ref, slots_ref = refs[:count], refs[count:-2], refs[-2], refs[-1]
    slots = slots_of(named_of(named_ref), slots_ref.shape[0], named_ref.shape[2])
    slots_ref[...] = slots
    normed = normed_of(other_ref[...], gain_ref[...])
    normed_ref[...] = normed
    packed = picked(section_ref[0], slots, normed, steps, per_expert)
    each = packed.shape[0] // count
    for place, (half_ref, out_ref) in enumerate(zip(half_refs, out_refs)):
        out_ref[:each, :] = half_ref[...]
        out_ref[each:, :] = packed[place * each : (place + 1) * each, :]


def other_part(section, other, named, gain, halves, steps, per_expert, experts):
    rows, width = other.shape
    shapes = [shaped(rows, width, jnp.bfloat16)] * (len(steps) + 1)
    shapes.append(shaped(experts, rows, jnp.float32))
    return pl.pallas_call(
        functools.partial(other_kernel, steps, per_expert),
        out_shape=shapes,
        in_specs=[SMEM] + [VMEM] * (3 + len(halves)),
        out_specs=[VMEM] * len(shapes),
        compiler_params=PARAMS,
        name="other_part",
    )(section, other, named, gain, *halves)


def mix_kernel(sets, per_expert, section_ref, normed_ref, slots_ref, named_ref, router_ref, *outs):
    experts, every = slots_ref.shape
    logits = lax.dot_general(
        normed_ref[...], router_ref[...], NT, preferred_element_type=jnp.float32
    )
    diagonal = lax.broadcasted_iota(jnp.int32, (every, every), 0) == (
        lax.broadcasted_iota(jnp.int32, (every, every), 1)
    )

    def upright(row):
        return jnp.sum(jnp.where(diagonal, row, 0.0), axis=1, keepdims=True)

    first, second = upright(named_ref[0:1, :]), upright(named_ref[1:2, :])
    ids = lax.broadcasted_iota(jnp.int32, logits.shape, 1).astype(jnp.float32)
    lead = jnp.sum(jnp.where(first == ids, logits, 0.0), axis=1, keepdims=True)
    trail = jnp.sum(jnp.where(second == ids, logits, 0.0), axis=1, keepdims=True)
    weight_a = 1.0 / (1.0 + jnp.exp(trail - lead))
    weight_b = 1.0 / (1.0 + jnp.exp(lead - trail))
    section = section_ref[0]
    tall = lax.broadcasted_iota(jnp.int32, (experts, every), 0).astype(jnp.float32)
    for place, distances in enumerate(sets):
        high_ref, low_ref = outs[2 * place : 2 * place + 2]
        count, width = high_ref.shape
        each = width // len(distances)
        lanes = lax.broadcasted_iota(jnp.int32, (count, width), 1).astype(jnp.float32)
        spread = jnp.zeros((count, width), jnp.float32)
        for at, distance in enumerate(distances):
            expert = expert_at(section, distance, per_expert)
            slot = jnp.sum(jnp.where(tall == expert, slots_ref[...], 0.0), axis=0, keepdims=True)
            weight = jnp.where(first == expert, weight_a, 0.0) + jnp.where(
                second == expert, weight_b, 0.0
            )
            spread = spread + jnp.where(
                upright(slot) + at * each == lanes, weight, 0.0
            )
        high = spread.astype(jnp.bfloat16)
        high_ref[...] = high
        low_ref[...] = (spread - high.astype(jnp.float32)).astype(jnp.bfloat16)


def mix(section, normed, slots, named, router, early, near, per_expert):
    rows = normed.shape[0]
    shapes = [
        shaped(rows, len(distances) * rows // 2, jnp.bfloat16)
        for distances in (early, near)
        for _ in range(2)
    ]
    return pl.pallas_call(
        functools.partial(mix_kernel, (early, near), per_expert),
        out_shape=shapes,
        in_specs=[SMEM] + [VMEM] * 4,
        out_specs=[VMEM] * len(shapes),
        compiler_params=PARAMS,
        name="mix",
    )(section, normed, slots, named, router)


def load_kernel(count, steps, per_expert, section_ref, in_ref, *refs):
    sources, refs = refs[:count], refs[count:]
    normed_refs, slots_refs, refs = refs[:2], refs[2:4], refs[4:]
    turned_ref, targets, out_refs = refs[0], refs[1 : 1 + count], refs[1 + count : -2]
    held_ref, sems = refs[-2:]
    pieces, rows, _ = held_ref.shape
    copies = [
        pltpu.make_async_copy(in_ref.at[pl.ds(k * rows, rows)], held_ref.at[k], sems.at[k])
        for k in range(pieces)
    ]
    others = [
        pltpu.make_async_copy(source, target, sems.at[pieces + k])
        for k, (source, target) in enumerate(zip(sources, targets))
    ]
    for copy in copies + others:
        copy.start()
    for part, (normed_ref, slots_ref) in enumerate(zip(normed_refs, slots_refs)):
        packed = picked(section_ref[0], slots_ref[...], normed_ref[...], steps, per_expert)
        each = packed.shape[0] // len(steps)
        for place, out_ref in enumerate(out_refs):
            out_ref[part * each : (part + 1) * each, :] = packed[
                place * each : (place + 1) * each, :
            ]
    for k in range(pieces):
        copies[k].wait()
        turned_ref[:, k * rows : (k + 1) * rows] = held_ref[k].T
    for copy in others:
        copy.wait()


def load_weights(section, stacked_in, others, normed, slots, steps, per_expert):
    count = len(others)
    rows, width = stacked_in.shape
    pieces = max(1, rows // LANES)
    arrays = [pltpu.with_memory_space_constraint(a, pltpu.HBM) for a in (stacked_in, *others)]
    shapes = [shaped(width, rows, stacked_in.dtype)]
    shapes += [jax.ShapeDtypeStruct(a.shape, a.dtype) for a in others]
    shapes += [shaped(normed[0].shape[0], width, jnp.bfloat16)] * len(steps)
    return pl.pallas_call(
        functools.partial(load_kernel, count, steps, per_expert),
        out_shape=shapes,
        in_specs=[SMEM] + [HBM] * (count + 1) + [VMEM] * 4,
        out_specs=[VMEM] * len(shapes),
        scratch_shapes=[
            pltpu.VMEM((pieces, rows // pieces, width), stacked_in.dtype),
            pltpu.SemaphoreType.DMA((pieces + count,)),
        ],
        compiler_params=PARAMS,
        name="load_weights",
    )(section, *arrays, *normed, *slots)


def expert_kernel(count, after, in_ref, down_ref, *refs):
    blocks, every_ref = refs[:count], refs[-1]
    out_refs = refs[count + after : -1]
    every = gathered(blocks, every_ref)
    gate_up = jnp.dot(every, in_ref[...], preferred_element_type=jnp.float32)
    hidden = gate_up.shape[1] // 2
    gate = gate_up[:, :hidden]
    active = (gate / (1.0 + jnp.exp(-gate)) * gate_up[:, hidden:]).astype(jnp.bfloat16)
    partial = jnp.dot(active, down_ref[...], preferred_element_type=jnp.float32)
    rows = out_refs[0].shape[0]
    for place, out_ref in enumerate(out_refs):
        out_ref[...] = partial[place * rows : (place + 1) * rows, :].astype(jnp.bfloat16)


def run_expert(blocks, turned_in, down, pieces, after=()):
    count = len(blocks)
    rows, width = blocks[0].shape
    return pl.pallas_call(
        functools.partial(expert_kernel, count, len(after)),
        out_shape=[shaped(rows // pieces, width, jnp.bfloat16)] * (count * pieces),
        in_specs=[VMEM] * (2 + count) + [ANY] * len(after),
        out_specs=[VMEM] * (count * pieces),
        scratch_shapes=[pltpu.VMEM((count * rows, width), jnp.bfloat16)],
        compiler_params=PARAMS,
        name="expert",
    )(turned_in, down, *blocks, *after)


def gathered(blocks, every_ref):
    rows = blocks[0].shape[0]
    for place, block in enumerate(blocks):
        every_ref[place * rows : (place + 1) * rows, :] = block[...]
    return every_ref[...]


def begin_kernel(count, high_ref, low_ref, *refs):
    blocks, out_ref, every_ref = refs[:count], refs[count], refs[-1]
    every = gathered(blocks, every_ref)
    total = jnp.dot(low_ref[...], every, preferred_element_type=jnp.float32)
    out_ref[...] = total + jnp.dot(high_ref[...], every, preferred_element_type=jnp.float32)


def begin(high, low, blocks):
    count = len(blocks)
    each, width = blocks[0].shape
    return pl.pallas_call(
        functools.partial(begin_kernel, count),
        out_shape=shaped(high.shape[0], width, jnp.float32),
        in_specs=[VMEM] * (2 + count),
        out_specs=VMEM,
        scratch_shapes=[pltpu.VMEM((count * each, width), jnp.bfloat16)],
        compiler_params=PARAMS,
        name="begin",
    )(high, low, *blocks)


def close_kernel(count, targets, member_ref, tokens_ref, high_ref, low_ref, begun_ref, *refs):
    blocks, outs, every_ref, total_ref = refs[:count], refs[count:-2], refs[-2], refs[-1]
    every = gathered(blocks, every_ref)
    total = begun_ref[...] + jnp.dot(low_ref[...], every, preferred_element_type=jnp.float32)
    total_ref[...] = total + jnp.dot(high_ref[...], every, preferred_element_type=jnp.float32)
    if len(outs) == 1:
        outs[0][...] = total_ref[...]
        return
    part = outs[0].shape[1]
    for k, out_ref in enumerate(outs):
        place = target_of(member_ref[0], targets[k - 1]) if k else member_ref[0]
        columns = pl.ds(pl.multiple_of(place * part, LANES), part)
        value = total_ref[:, columns]
        if k == 0:
            value = value + tokens_ref[:, columns].astype(jnp.float32)
        out_ref[...] = value.astype(out_ref.dtype)


def close(high, low, begun, blocks, tokens, member, inner_count):
    count = len(blocks)
    each = blocks[0].shape[0]
    rows, width = begun.shape
    part = width // inner_count
    whole = part % LANES != 0
    targets = inner_targets(inner_count)
    kinds = [jnp.float32] + [jnp.bfloat16] * (inner_count - 1)
    shapes = [shaped(rows, part, kind) for kind in kinds]
    if whole:
        shapes = [shaped(rows, width, jnp.float32)]
    outs = pl.pallas_call(
        functools.partial(close_kernel, count, targets),
        out_shape=shapes,
        in_specs=[SMEM] + [VMEM] * (4 + count),
        out_specs=[VMEM] * len(shapes),
        scratch_shapes=[
            pltpu.VMEM((count * each, width), jnp.bfloat16),
            pltpu.VMEM((rows, width), jnp.float32),
        ],
        compiler_params=PARAMS,
        name="close",
    )(member.reshape(1), tokens, high, low, begun, *blocks)
    if not whole:
        return outs
    rounded = outs[0].astype(jnp.bfloat16)
    total = outs[0] + tokens.astype(jnp.float32)
    outs = [lax.dynamic_slice_in_dim(total, member * part, part, 1)]
    for k in range(1, inner_count):
        place = target_of(member, targets[k - 1])
        outs.append(lax.dynamic_slice_in_dim(rounded, place * part, part, 1))
    return outs


def final_kernel(*refs):
    out_ref = refs[-1]
    micro, row_count, _ = out_ref.shape
    total = refs[0][...]
    for ref in refs[1:-1]:
        total = total + ref[...].astype(jnp.float32)
    for m in range(micro):
        out_ref[m] = total[m * row_count : (m + 1) * row_count].astype(out_ref.dtype)


def finish(pieces, micro, row_count):
    part = pieces[0].shape[1]
    return pl.pallas_call(
        final_kernel,
        out_shape=jax.ShapeDtypeStruct((micro, row_count, part), jnp.bfloat16),
        in_specs=[VMEM] * len(pieces),
        out_specs=VMEM,
        compiler_params=PARAMS,
        name="finish",
    )(*pieces)


def body(tokens, norm_gain, router, expert_in, expert_out, choices):
    sections = lax.axis_size("section")
    inner_count = lax.axis_size("inner")
    member = lax.axis_index("inner").astype(jnp.int32)
    section = lax.axis_index("section").astype(jnp.int32).reshape(1)
    chips = sections // 2
    experts = router.shape[1]
    per_expert = sections // experts
    micro, row_count, width = tokens.shape
    rows = micro * row_count
    hidden = expert_in.shape[2]
    own = tokens.reshape(rows, width)
    named = choices.transpose(0, 2, 1)
    gain = norm_gain.reshape(1, width)

    far = chips - 1
    first_steps = ((0, 0), (far, far))
    steps = []
    for k in range(1, far, 2):
        steps += [(k, k + 1), (k + 1, k)]

    other = trade(own, "section", 1)
    other_named = trade(named, "section", 1)
    *halves, own, gain, normed, slots, names = own_part(
        section, own, named, gain, first_steps, per_expert, experts
    )
    message, away, other_normed, other_slots = other_part(
        section, other, other_named, gain, halves, first_steps, per_expert, experts
    )
    away = visit(away, (far, far), 0)
    turned_in, router_rows, down, *messages = load_weights(
        section,
        expert_in[0].reshape(2 * hidden, width),
        (router.T, expert_out[0]),
        (normed, other_normed),
        (slots, other_slots),
        tuple(steps),
        per_expert,
    )
    arrived = [visit(value, step, 0) for value, step in zip(messages, steps)]

    def origins(step):
        a, b = step
        return ((2 * a, 2 * b), (2 * b + 1, 2 * a + 1))

    early = origins((far, far)) + origins((0, 0))
    late = tuple(pair for step in steps for pair in origins(step))
    high_a, low_a, high_b, low_b = mix(
        section, normed, slots, names, router_rows, early, late, per_expert
    )
    here, beside = run_expert([message], turned_in, down, 2)
    beside = trade(beside, "section", 1)
    away = run_expert([away], turned_in, down, 2, (here,))
    results = run_expert(arrived, turned_in, down, 2, (away[0],))
    away = [visit(value, (far, far), cross) for cross, value in enumerate(away)]
    begun = begin(high_a, low_a, [*away, here, beside])
    results = [visit(value, steps[j // 2], j % 2) for j, value in enumerate(results)]
    split = close(high_b, low_b, begun, results, own, member, inner_count)
    targets = inner_targets(inner_count)
    pieces = [split[0]] + [turn(value, order) for value, order in zip(split[1:], targets)]
    return finish(pieces, micro, row_count)


def solution(mesh):
    return jax.shard_map(
        body,
        mesh=mesh,
        in_specs=(
            P(None, "section", None),
            P(),
            P(),
            P("section", None, "inner", None),
            P("section", "inner", None),
            P(None, "section", None),
        ),
        out_specs=P(None, "section", "inner"),
        check_vma=False,
    )
```

```python
import functools

import jax
import jax.numpy as jnp
from jax import lax
from jax.experimental import pallas as pl
from jax.experimental.pallas import tpu as pltpu
from jax.sharding import PartitionSpec as P

epsilon = 1e-05
LANES = 128
FIRST = (0,)
INNER_STEPS = ((1, 2), (2, 1), (3, 3))
TOKEN_COPIES = 4
NT = (((1,), (1,)), ((), ()))
VMEM = pl.BlockSpec(memory_space=pltpu.VMEM)
ANY = pl.BlockSpec(memory_space=pl.ANY)
HBM = pl.BlockSpec(memory_space=pltpu.HBM)
SMEM = pl.BlockSpec(memory_space=pltpu.SMEM)
PARAMS = pltpu.CompilerParams(vmem_limit_bytes=20 * 1024 * 1024)


def trade(value, axis, distance):
    count = lax.axis_size(axis)
    return lax.ppermute(value, axis, [(place, place ^ distance) for place in range(count)])


def inner_steps(count):
    if count == len(INNER_STEPS) + 1:
        return INNER_STEPS
    return tuple((k, k) for k in range(1, count))


def place_after(member, section, step, count):
    return lax.rem(member + jnp.where(section % 2 == 0, step[0], step[1]), count)


def turn(value, step):
    sections, count = lax.axis_size("section"), lax.axis_size("inner")
    pairs = [
        (section * count + place, section * count + (place + step[section % 2]) % count)
        for section in range(sections)
        for place in range(count)
    ]
    return lax.ppermute(value, ("section", "inner"), pairs)


def visit(value, step, cross):
    count = lax.axis_size("section")
    pairs = [(place, place ^ (2 * step[place % 2]) ^ cross) for place in range(count)]
    return lax.ppermute(value, "section", pairs)


def shaped(rows, width, dtype):
    return jax.ShapeDtypeStruct((rows, width), dtype)


def expert_at(section, distances, per_expert):
    distance = jnp.where(section % 2 == 0, distances[0], distances[1])
    return lax.div(section ^ distance, jnp.int32(per_expert)).astype(jnp.float32)


def slots_of(named, experts, row_count):
    rows = named[0].shape[1]
    ids = lax.broadcasted_iota(jnp.int32, (experts, rows), 0).astype(jnp.float32)
    hit = (named[0] == ids) | (named[1] == ids)
    above = lax.broadcasted_iota(jnp.int32, (rows, rows), 0)
    column = lax.broadcasted_iota(jnp.int32, (rows, rows), 1)
    earlier = (above < column) & (above // row_count == column // row_count)
    rank = jnp.dot(
        hit.astype(jnp.bfloat16), earlier.astype(jnp.bfloat16), preferred_element_type=jnp.float32
    )
    group = lax.broadcasted_iota(jnp.int32, (experts, rows), 1) // row_count
    return jnp.where(hit, (group * (row_count // 2)).astype(jnp.float32) + rank, -1.0)


def picked(section, slots, normed, steps, per_expert):
    experts, rows = slots.shape
    ids = lax.broadcasted_iota(jnp.int32, (experts, rows), 0).astype(jnp.float32)
    slot_ids = lax.broadcasted_iota(jnp.int32, (rows // 2, rows), 0).astype(jnp.float32)
    picks = []
    for step in steps:
        expert = expert_at(section, (2 * step[0], 2 * step[1]), per_expert)
        slot = jnp.sum(jnp.where(ids == expert, slots, 0.0), axis=0, keepdims=True)
        picks.append(jnp.where(slot == slot_ids, 1.0, 0.0))
    pick = jnp.concatenate(picks, axis=0).astype(jnp.bfloat16)
    return jnp.dot(pick, normed, preferred_element_type=jnp.float32).astype(jnp.bfloat16)


def normed_of(values, gain):
    values = values.astype(jnp.float32)
    inv_rms = lax.rsqrt(jnp.mean(values * values, axis=-1, keepdims=True) + epsilon)
    return (values * inv_rms * gain).astype(jnp.bfloat16)


def named_of(ref):
    micro = ref.shape[0]
    return [
        jnp.concatenate([ref[m, k : k + 1, :] for m in range(micro)], axis=1).astype(jnp.float32)
        for k in range(2)
    ]


def own_kernel(steps, per_expert, section_ref, tokens_ref, named_ref, gain_ref, *refs):
    half_refs, refs = refs[: len(steps)], refs[len(steps) :]
    own_ref, gain_out_ref, normed_ref, slots_ref, names_ref, held_ref, sems = refs
    width = tokens_ref.shape[1]
    chunk = width // TOKEN_COPIES
    spans = [pl.ds(k * chunk, chunk) for k in range(TOKEN_COPIES)]
    pairs = [(tokens_ref.at[:, span], own_ref.at[:, span]) for span in spans]
    pairs = [(named_ref, held_ref), *pairs, (gain_ref, gain_out_ref)]
    copies = [
        pltpu.make_async_copy(source, target, sems.at[k])
        for k, (source, target) in enumerate(pairs)
    ]
    for copy in copies:
        copy.start()
    copies[0].wait()
    named = named_of(held_ref)
    slots = slots_of(named, slots_ref.shape[0], named_ref.shape[2])
    slots_ref[...] = slots
    names_ref[0:1, :] = named[0]
    names_ref[1:2, :] = named[1]
    for copy in copies[1:]:
        copy.wait()
    normed = normed_of(own_ref[...], gain_out_ref[...])
    normed_ref[...] = normed
    packed = picked(section_ref[0], slots, normed, steps, per_expert)
    each = packed.shape[0] // len(steps)
    for place, half_ref in enumerate(half_refs):
        half_ref[...] = packed[place * each : (place + 1) * each, :]


def own_part(section, tokens, named, gain, steps, per_expert, experts):
    rows, width = tokens.shape
    arrays = [pltpu.with_memory_space_constraint(a, pltpu.HBM) for a in (tokens, named, gain)]
    shapes = [shaped(rows // 2, width, jnp.bfloat16)] * len(steps) + [
        shaped(rows, width, jnp.bfloat16),
        shaped(1, width, jnp.float32),
        shaped(rows, width, jnp.bfloat16),
        shaped(experts, rows, jnp.float32),
        shaped(2, rows, jnp.float32),
    ]
    return pl.pallas_call(
        functools.partial(own_kernel, steps, per_expert),
        out_shape=shapes,
        in_specs=[SMEM] + [HBM] * 3,
        out_specs=[VMEM] * len(shapes),
        scratch_shapes=[pltpu.VMEM(named.shape, jnp.int32), pltpu.SemaphoreType.DMA((TOKEN_COPIES + 2,))],
        compiler_params=PARAMS,
        name="own_part",
    )(section, *arrays)


def other_kernel(steps, per_expert, section_ref, other_ref, named_ref, gain_ref, *refs):
    count = len(steps)
    half_refs, out_refs, normed_ref, slots_ref = refs[:count], refs[count:-2], refs[-2], refs[-1]
    slots = slots_of(named_of(named_ref), slots_ref.shape[0], named_ref.shape[2])
    slots_ref[...] = slots
    normed = normed_of(other_ref[...], gain_ref[...])
    normed_ref[...] = normed
    packed = picked(section_ref[0], slots, normed, steps, per_expert)
    each = packed.shape[0] // count
    for place, (half_ref, out_ref) in enumerate(zip(half_refs, out_refs)):
        out_ref[:each, :] = half_ref[...]
        out_ref[each:, :] = packed[place * each : (place + 1) * each, :]


def other_part(section, other, named, gain, halves, steps, per_expert, experts):
    rows, width = other.shape
    shapes = [shaped(rows, width, jnp.bfloat16)] * (len(steps) + 1)
    shapes.append(shaped(experts, rows, jnp.float32))
    return pl.pallas_call(
        functools.partial(other_kernel, steps, per_expert),
        out_shape=shapes,
        in_specs=[SMEM] + [VMEM] * (3 + len(halves)),
        out_specs=[VMEM] * len(shapes),
        compiler_params=PARAMS,
        name="other_part",
    )(section, other, named, gain, *halves)


def mix_kernel(sets, per_expert, section_ref, normed_ref, slots_ref, named_ref, router_ref, *outs):
    experts, every = slots_ref.shape
    logits = lax.dot_general(
        normed_ref[...], router_ref[...], NT, preferred_element_type=jnp.float32
    )
    diagonal = lax.broadcasted_iota(jnp.int32, (every, every), 0) == (
        lax.broadcasted_iota(jnp.int32, (every, every), 1)
    )

    def upright(row):
        return jnp.sum(jnp.where(diagonal, row, 0.0), axis=1, keepdims=True)

    first, second = upright(named_ref[0:1, :]), upright(named_ref[1:2, :])
    ids = lax.broadcasted_iota(jnp.int32, logits.shape, 1).astype(jnp.float32)
    lead = jnp.sum(jnp.where(first == ids, logits, 0.0), axis=1, keepdims=True)
    trail = jnp.sum(jnp.where(second == ids, logits, 0.0), axis=1, keepdims=True)
    weight_a = 1.0 / (1.0 + jnp.exp(trail - lead))
    weight_b = 1.0 / (1.0 + jnp.exp(lead - trail))
    section = section_ref[0]
    tall = lax.broadcasted_iota(jnp.int32, (experts, every), 0).astype(jnp.float32)
    for place, distances in enumerate(sets):
        out_ref = outs[place]
        count, width = out_ref.shape[0], out_ref.shape[1] // 2
        each = width // len(distances)
        lanes = lax.broadcasted_iota(jnp.int32, (count, width), 1).astype(jnp.float32)
        spread = jnp.zeros((count, width), jnp.float32)
        for at, distance in enumerate(distances):
            expert = expert_at(section, distance, per_expert)
            slot = jnp.sum(jnp.where(tall == expert, slots_ref[...], 0.0), axis=0, keepdims=True)
            weight = jnp.where(first == expert, weight_a, 0.0) + jnp.where(
                second == expert, weight_b, 0.0
            )
            spread = spread + jnp.where(
                upright(slot) + at * each == lanes, weight, 0.0
            )
        high = spread.astype(jnp.bfloat16)
        low = (spread - high.astype(jnp.float32)).astype(jnp.bfloat16)
        out_ref[...] = jnp.concatenate([high, low], axis=1)


def mix(section, normed, slots, named, router, early, near, per_expert):
    rows = normed.shape[0]
    shapes = [
        shaped(rows, len(distances) * rows, jnp.bfloat16) for distances in (early, near)
    ]
    return pl.pallas_call(
        functools.partial(mix_kernel, (early, near), per_expert),
        out_shape=shapes,
        in_specs=[SMEM] + [VMEM] * 4,
        out_specs=[VMEM] * len(shapes),
        compiler_params=PARAMS,
        name="mix",
    )(section, normed, slots, named, router)


def load_kernel(count, steps, per_expert, section_ref, in_ref, *refs):
    sources, refs = refs[:count], refs[count:]
    normed_refs, slots_refs, refs = refs[:2], refs[2:4], refs[4:]
    turned_ref, targets, out_refs = refs[0], refs[1 : 1 + count], refs[1 + count : -2]
    held_ref, sems = refs[-2:]
    pieces, rows, _ = held_ref.shape
    copies = [
        pltpu.make_async_copy(in_ref.at[pl.ds(k * rows, rows)], held_ref.at[k], sems.at[k])
        for k in range(pieces)
    ]
    others = [
        pltpu.make_async_copy(source, target, sems.at[pieces + k])
        for k, (source, target) in enumerate(zip(sources, targets))
    ]
    for copy in copies + others:
        copy.start()
    for part, (normed_ref, slots_ref) in enumerate(zip(normed_refs, slots_refs)):
        packed = picked(section_ref[0], slots_ref[...], normed_ref[...], steps, per_expert)
        each = packed.shape[0] // len(steps)
        for place, out_ref in enumerate(out_refs):
            out_ref[part * each : (part + 1) * each, :] = packed[
                place * each : (place + 1) * each, :
            ]
    for k in range(pieces):
        copies[k].wait()
        turned_ref[:, k * rows : (k + 1) * rows] = held_ref[k].T
    for copy in others:
        copy.wait()


def load_weights(section, stacked_in, others, normed, slots, steps, per_expert):
    count = len(others)
    rows, width = stacked_in.shape
    pieces = max(1, rows // LANES)
    arrays = [pltpu.with_memory_space_constraint(a, pltpu.HBM) for a in (stacked_in, *others)]
    shapes = [shaped(width, rows, stacked_in.dtype)]
    shapes += [jax.ShapeDtypeStruct(a.shape, a.dtype) for a in others]
    shapes += [shaped(normed[0].shape[0], width, jnp.bfloat16)] * len(steps)
    return pl.pallas_call(
        functools.partial(load_kernel, count, steps, per_expert),
        out_shape=shapes,
        in_specs=[SMEM] + [HBM] * (count + 1) + [VMEM] * 4,
        out_specs=[VMEM] * len(shapes),
        scratch_shapes=[
            pltpu.VMEM((pieces, rows // pieces, width), stacked_in.dtype),
            pltpu.SemaphoreType.DMA((pieces + count,)),
        ],
        compiler_params=PARAMS,
        name="load_weights",
    )(section, *arrays, *normed, *slots)


def expert_kernel(count, after, in_ref, down_ref, *refs):
    blocks, every_ref = refs[:count], refs[-1]
    out_refs = refs[count + after : -1]
    every = gathered(blocks, every_ref)
    gate_up = jnp.dot(every, in_ref[...], preferred_element_type=jnp.float32)
    hidden = gate_up.shape[1] // 2
    gate = gate_up[:, :hidden]
    active = (gate / (1.0 + jnp.exp(-gate)) * gate_up[:, hidden:]).astype(jnp.bfloat16)
    partial = jnp.dot(active, down_ref[...], preferred_element_type=jnp.float32)
    rows = out_refs[0].shape[0]
    for place, out_ref in enumerate(out_refs):
        out_ref[...] = partial[place * rows : (place + 1) * rows, :].astype(jnp.bfloat16)


def run_expert(blocks, turned_in, down, pieces, after=()):
    count = len(blocks)
    rows, width = blocks[0].shape
    return pl.pallas_call(
        functools.partial(expert_kernel, count, len(after)),
        out_shape=[shaped(rows // pieces, width, jnp.bfloat16)] * (count * pieces),
        in_specs=[VMEM] * (2 + count) + [ANY] * len(after),
        out_specs=[VMEM] * (count * pieces),
        scratch_shapes=[pltpu.VMEM((count * rows, width), jnp.bfloat16)],
        compiler_params=PARAMS,
        name="expert",
    )(turned_in, down, *blocks, *after)


def gathered(blocks, every_ref):
    rows = blocks[0].shape[0]
    for place, block in enumerate(blocks):
        every_ref[place * rows : (place + 1) * rows, :] = block[...]
    return every_ref[...]


def weighed(weights_ref, blocks, every_ref):
    gathered((*blocks, *blocks), every_ref)
    return jnp.dot(weights_ref[...], every_ref[...], preferred_element_type=jnp.float32)


def begin_kernel(count, weights_ref, *refs):
    blocks, out_ref, every_ref = refs[:count], refs[count], refs[-1]
    out_ref[...] = weighed(weights_ref, blocks, every_ref)


def begin(weights, blocks):
    count = len(blocks)
    each, width = blocks[0].shape
    return pl.pallas_call(
        functools.partial(begin_kernel, count),
        out_shape=shaped(weights.shape[0], width, jnp.float32),
        in_specs=[VMEM] * (1 + count),
        out_specs=VMEM,
        scratch_shapes=[pltpu.VMEM((2 * count * each, width), jnp.bfloat16)],
        compiler_params=PARAMS,
        name="begin",
    )(weights, *blocks)


def close_kernel(count, steps, member_ref, section_ref, tokens_ref, weights_ref, begun_ref, *refs):
    blocks, outs, every_ref, total_ref = refs[:count], refs[count:-2], refs[-2], refs[-1]
    total_ref[...] = begun_ref[...] + weighed(weights_ref, blocks, every_ref)
    if len(outs) == 1:
        outs[0][...] = total_ref[...]
        return
    part = outs[0].shape[1]
    for k, out_ref in enumerate(outs):
        place = member_ref[0]
        if k:
            place = place_after(place, section_ref[0], steps[k - 1], len(outs))
        columns = pl.ds(pl.multiple_of(place * part, LANES), part)
        value = total_ref[:, columns]
        if k == 0:
            value = value + tokens_ref[:, columns].astype(jnp.float32)
        out_ref[...] = value.astype(out_ref.dtype)


def close(weights, begun, blocks, tokens, member, section, inner_count):
    count = len(blocks)
    each = blocks[0].shape[0]
    rows, width = begun.shape
    part = width // inner_count
    whole = part % LANES != 0
    steps = inner_steps(inner_count)
    kinds = [jnp.float32] + [jnp.bfloat16] * (inner_count - 1)
    shapes = [shaped(rows, part, kind) for kind in kinds]
    if whole:
        shapes = [shaped(rows, width, jnp.float32)]
    outs = pl.pallas_call(
        functools.partial(close_kernel, count, steps),
        out_shape=shapes,
        in_specs=[SMEM] * 2 + [VMEM] * (3 + count),
        out_specs=[VMEM] * len(shapes),
        scratch_shapes=[
            pltpu.VMEM((2 * count * each, width), jnp.bfloat16),
            pltpu.VMEM((rows, width), jnp.float32),
        ],
        compiler_params=PARAMS,
        name="close",
    )(member.reshape(1), section, tokens, weights, begun, *blocks)
    if not whole:
        return outs
    rounded = outs[0].astype(jnp.bfloat16)
    total = outs[0] + tokens.astype(jnp.float32)
    outs = [lax.dynamic_slice_in_dim(total, member * part, part, 1)]
    for k in range(1, inner_count):
        place = place_after(member, section[0], steps[k - 1], inner_count)
        outs.append(lax.dynamic_slice_in_dim(rounded, place * part, part, 1))
    return outs


def final_kernel(*refs):
    out_ref = refs[-1]
    micro, row_count, _ = out_ref.shape
    total = refs[0][...]
    for ref in refs[1:-1]:
        total = total + ref[...].astype(jnp.float32)
    for m in range(micro):
        out_ref[m] = total[m * row_count : (m + 1) * row_count].astype(out_ref.dtype)


def finish(pieces, micro, row_count):
    part = pieces[0].shape[1]
    return pl.pallas_call(
        final_kernel,
        out_shape=jax.ShapeDtypeStruct((micro, row_count, part), jnp.bfloat16),
        in_specs=[VMEM] * len(pieces),
        out_specs=VMEM,
        compiler_params=PARAMS,
        name="finish",
    )(*pieces)


def body(tokens, norm_gain, router, expert_in, expert_out, choices):
    sections = lax.axis_size("section")
    inner_count = lax.axis_size("inner")
    member = lax.axis_index("inner").astype(jnp.int32)
    section = lax.axis_index("section").astype(jnp.int32).reshape(1)
    chips = sections // 2
    experts = router.shape[1]
    per_expert = sections // experts
    micro, row_count, width = tokens.shape
    rows = micro * row_count
    hidden = expert_in.shape[2]
    own = tokens.reshape(rows, width)
    named = choices.transpose(0, 2, 1)
    gain = norm_gain.reshape(1, width)

    far = chips - 1
    steps = [(far, far)]
    for k in range(1, far, 2):
        steps += [(k, k + 1), (k + 1, k)]
    first = [steps[k] for k in FIRST]
    second = [step for step in steps if step not in first]
    first_steps = ((0, 0), *first)

    other = trade(own, "section", 1)
    other_named = trade(named, "section", 1)
    *halves, own, gain, normed, slots, names = own_part(
        section, own, named, gain, first_steps, per_expert, experts
    )
    message, *messages, other_normed, other_slots = other_part(
        section, other, other_named, gain, halves, first_steps, per_expert, experts
    )
    first_blocks = [visit(value, step, 0) for value, step in zip(messages, first)]
    turned_in, router_rows, down, *messages = load_weights(
        section,
        expert_in[0].reshape(2 * hidden, width),
        (router.T, expert_out[0]),
        (normed, other_normed),
        (slots, other_slots),
        tuple(second),
        per_expert,
    )
    second_blocks = [visit(value, step, 0) for value, step in zip(messages, second)]

    def origins(step):
        a, b = step
        return ((2 * a, 2 * b), (2 * b + 1, 2 * a + 1))

    def send_back(results, steps):
        return [visit(value, steps[j // 2], j % 2) for j, value in enumerate(results)]

    early = tuple(pair for step in (*first, (0, 0)) for pair in origins(step))
    late = tuple(pair for step in second for pair in origins(step))
    early_weights, late_weights = mix(
        section, normed, slots, names, router_rows, early, late, per_expert
    )
    here, beside = run_expert([message], turned_in, down, 2)
    beside = trade(beside, "section", 1)
    first_results = run_expert(first_blocks, turned_in, down, 2, (here,))
    second_results = run_expert(second_blocks, turned_in, down, 2, (first_results[0],))
    begun = begin(early_weights, [*send_back(first_results, first), here, beside])
    split = close(
        late_weights,
        begun,
        send_back(second_results, second),
        own,
        member,
        section,
        inner_count,
    )
    pieces = [split[0]]
    pieces += [turn(value, step) for value, step in zip(split[1:], inner_steps(inner_count))]
    return finish(pieces, micro, row_count)


def solution(mesh):
    return jax.shard_map(
        body,
        mesh=mesh,
        in_specs=(
            P(None, "section", None),
            P(),
            P(),
            P("section", None, "inner", None),
            P("section", "inner", None),
            P(None, "section", None),
        ),
        out_specs=P(None, "section", "inner"),
        check_vma=False,
    )
```

```python
import functools

import jax
import jax.numpy as jnp
from jax import lax
from jax.experimental import pallas as pl
from jax.experimental.pallas import tpu as pltpu
from jax.sharding import PartitionSpec as P

epsilon = 1e-05
LANES = 128
INNER_ORDER = ((1, 2, 3, 0), (2, 3, 0, 1), (3, 0, 1, 2))
TOKEN_COPIES = 4
NT = (((1,), (1,)), ((), ()))
VMEM = pl.BlockSpec(memory_space=pltpu.VMEM)
ANY = pl.BlockSpec(memory_space=pl.ANY)
HBM = pl.BlockSpec(memory_space=pltpu.HBM)
SMEM = pl.BlockSpec(memory_space=pltpu.SMEM)
PARAMS = pltpu.CompilerParams(vmem_limit_bytes=20 * 1024 * 1024)


def trade(value, axis, distance):
    count = lax.axis_size(axis)
    return lax.ppermute(value, axis, [(place, place ^ distance) for place in range(count)])


def inner_targets(count):
    if count == len(INNER_ORDER[0]):
        return INNER_ORDER
    return tuple(
        tuple((place + k) % count for place in range(count)) for k in range(1, count)
    )


def target_of(member, targets):
    return sum(jnp.where(member == place, target, 0) for place, target in enumerate(targets))


def turn(value, targets):
    return lax.ppermute(value, "inner", list(enumerate(targets)))


def visit(value, step, cross):
    count = lax.axis_size("section")
    pairs = [(place, place ^ (2 * step[place % 2]) ^ cross) for place in range(count)]
    return lax.ppermute(value, "section", pairs)


def shaped(rows, width, dtype):
    return jax.ShapeDtypeStruct((rows, width), dtype)


def expert_at(section, distances, per_expert):
    distance = jnp.where(section % 2 == 0, distances[0], distances[1])
    return lax.div(section ^ distance, jnp.int32(per_expert)).astype(jnp.float32)


def slots_of(named, experts, row_count):
    rows = named[0].shape[1]
    ids = lax.broadcasted_iota(jnp.int32, (experts, rows), 0).astype(jnp.float32)
    hit = (named[0] == ids) | (named[1] == ids)
    above = lax.broadcasted_iota(jnp.int32, (rows, rows), 0)
    column = lax.broadcasted_iota(jnp.int32, (rows, rows), 1)
    earlier = (above < column) & (above // row_count == column // row_count)
    rank = jnp.dot(
        hit.astype(jnp.bfloat16), earlier.astype(jnp.bfloat16), preferred_element_type=jnp.float32
    )
    group = lax.broadcasted_iota(jnp.int32, (experts, rows), 1) // row_count
    return jnp.where(hit, (group * (row_count // 2)).astype(jnp.float32) + rank, -1.0)


def picked(section, slots, normed, steps, per_expert):
    experts, rows = slots.shape
    ids = lax.broadcasted_iota(jnp.int32, (experts, rows), 0).astype(jnp.float32)
    slot_ids = lax.broadcasted_iota(jnp.int32, (rows // 2, rows), 0).astype(jnp.float32)
    picks = []
    for step in steps:
        expert = expert_at(section, (2 * step[0], 2 * step[1]), per_expert)
        slot = jnp.sum(jnp.where(ids == expert, slots, 0.0), axis=0, keepdims=True)
        picks.append(jnp.where(slot == slot_ids, 1.0, 0.0))
    pick = jnp.concatenate(picks, axis=0).astype(jnp.bfloat16)
    return jnp.dot(pick, normed, preferred_element_type=jnp.float32).astype(jnp.bfloat16)


def normed_of(values, gain):
    values = values.astype(jnp.float32)
    inv_rms = lax.rsqrt(jnp.mean(values * values, axis=-1, keepdims=True) + epsilon)
    return (values * inv_rms * gain).astype(jnp.bfloat16)


def named_of(ref):
    micro = ref.shape[0]
    return [
        jnp.concatenate([ref[m, k : k + 1, :] for m in range(micro)], axis=1).astype(jnp.float32)
        for k in range(2)
    ]


def own_kernel(steps, per_expert, section_ref, tokens_ref, named_ref, gain_ref, *refs):
    half_refs, refs = refs[: len(steps)], refs[len(steps) :]
    own_ref, gain_out_ref, normed_ref, slots_ref, names_ref, held_ref, sems = refs
    width = tokens_ref.shape[1]
    chunk = width // TOKEN_COPIES
    spans = [pl.ds(k * chunk, chunk) for k in range(TOKEN_COPIES)]
    pairs = [(tokens_ref.at[:, span], own_ref.at[:, span]) for span in spans]
    pairs = [(named_ref, held_ref), *pairs, (gain_ref, gain_out_ref)]
    copies = [
        pltpu.make_async_copy(source, target, sems.at[k])
        for k, (source, target) in enumerate(pairs)
    ]
    for copy in copies:
        copy.start()
    copies[0].wait()
    named = named_of(held_ref)
    slots = slots_of(named, slots_ref.shape[0], named_ref.shape[2])
    slots_ref[...] = slots
    names_ref[0:1, :] = named[0]
    names_ref[1:2, :] = named[1]
    for copy in copies[1:]:
        copy.wait()
    normed = normed_of(own_ref[...], gain_out_ref[...])
    normed_ref[...] = normed
    packed = picked(section_ref[0], slots, normed, steps, per_expert)
    each = packed.shape[0] // len(steps)
    for place, half_ref in enumerate(half_refs):
        half_ref[...] = packed[place * each : (place + 1) * each, :]


def own_part(section, tokens, named, gain, steps, per_expert, experts):
    rows, width = tokens.shape
    arrays = [pltpu.with_memory_space_constraint(a, pltpu.HBM) for a in (tokens, named, gain)]
    shapes = [shaped(rows // 2, width, jnp.bfloat16)] * len(steps) + [
        shaped(rows, width, jnp.bfloat16),
        shaped(1, width, jnp.float32),
        shaped(rows, width, jnp.bfloat16),
        shaped(experts, rows, jnp.float32),
        shaped(2, rows, jnp.float32),
    ]
    return pl.pallas_call(
        functools.partial(own_kernel, steps, per_expert),
        out_shape=shapes,
        in_specs=[SMEM] + [HBM] * 3,
        out_specs=[VMEM] * len(shapes),
        scratch_shapes=[pltpu.VMEM(named.shape, jnp.int32), pltpu.SemaphoreType.DMA((TOKEN_COPIES + 2,))],
        compiler_params=PARAMS,
        name="own_part",
    )(section, *arrays)


def other_kernel(steps, per_expert, section_ref, other_ref, named_ref, gain_ref, *refs):
    count = len(steps)
    half_refs, out_refs, normed_ref, slots_ref = refs[:count], refs[count:-2], refs[-2], refs[-1]
    slots = slots_of(named_of(named_ref), slots_ref.shape[0], named_ref.shape[2])
    slots_ref[...] = slots
    normed = normed_of(other_ref[...], gain_ref[...])
    normed_ref[...] = normed
    packed = picked(section_ref[0], slots, normed, steps, per_expert)
    each = packed.shape[0] // count
    for place, (half_ref, out_ref) in enumerate(zip(half_refs, out_refs)):
        out_ref[:each, :] = half_ref[...]
        out_ref[each:, :] = packed[place * each : (place + 1) * each, :]


def other_part(section, other, named, gain, halves, steps, per_expert, experts):
    rows, width = other.shape
    shapes = [shaped(rows, width, jnp.bfloat16)] * (len(steps) + 1)
    shapes.append(shaped(experts, rows, jnp.float32))
    return pl.pallas_call(
        functools.partial(other_kernel, steps, per_expert),
        out_shape=shapes,
        in_specs=[SMEM] + [VMEM] * (3 + len(halves)),
        out_specs=[VMEM] * len(shapes),
        compiler_params=PARAMS,
        name="other_part",
    )(section, other, named, gain, *halves)


def mix_kernel(sets, per_expert, section_ref, normed_ref, slots_ref, named_ref, router_ref, *outs):
    experts, every = slots_ref.shape
    logits = lax.dot_general(
        normed_ref[...], router_ref[...], NT, preferred_element_type=jnp.float32
    )
    diagonal = lax.broadcasted_iota(jnp.int32, (every, every), 0) == (
        lax.broadcasted_iota(jnp.int32, (every, every), 1)
    )

    def upright(row):
        return jnp.sum(jnp.where(diagonal, row, 0.0), axis=1, keepdims=True)

    first, second = upright(named_ref[0:1, :]), upright(named_ref[1:2, :])
    ids = lax.broadcasted_iota(jnp.int32, logits.shape, 1).astype(jnp.float32)
    lead = jnp.sum(jnp.where(first == ids, logits, 0.0), axis=1, keepdims=True)
    trail = jnp.sum(jnp.where(second == ids, logits, 0.0), axis=1, keepdims=True)
    weight_a = 1.0 / (1.0 + jnp.exp(trail - lead))
    weight_b = 1.0 / (1.0 + jnp.exp(lead - trail))
    section = section_ref[0]
    tall = lax.broadcasted_iota(jnp.int32, (experts, every), 0).astype(jnp.float32)
    for place, distances in enumerate(sets):
        high_ref, low_ref = outs[2 * place : 2 * place + 2]
        count, width = high_ref.shape
        each = width // len(distances)
        lanes = lax.broadcasted_iota(jnp.int32, (count, width), 1).astype(jnp.float32)
        spread = jnp.zeros((count, width), jnp.float32)
        for at, distance in enumerate(distances):
            expert = expert_at(section, distance, per_expert)
            slot = jnp.sum(jnp.where(tall == expert, slots_ref[...], 0.0), axis=0, keepdims=True)
            weight = jnp.where(first == expert, weight_a, 0.0) + jnp.where(
                second == expert, weight_b, 0.0
            )
            spread = spread + jnp.where(
                upright(slot) + at * each == lanes, weight, 0.0
            )
        high = spread.astype(jnp.bfloat16)
        high_ref[...] = high
        low_ref[...] = (spread - high.astype(jnp.float32)).astype(jnp.bfloat16)


def mix(section, normed, slots, named, router, sets, per_expert):
    rows = normed.shape[0]
    shapes = [
        shaped(rows, len(distances) * rows // 2, jnp.bfloat16)
        for distances in sets
        for _ in range(2)
    ]
    return pl.pallas_call(
        functools.partial(mix_kernel, sets, per_expert),
        out_shape=shapes,
        in_specs=[SMEM] + [VMEM] * 4,
        out_specs=[VMEM] * len(shapes),
        compiler_params=PARAMS,
        name="mix",
    )(section, normed, slots, named, router)


def load_kernel(count, steps, per_expert, section_ref, in_ref, *refs):
    sources, refs = refs[:count], refs[count:]
    normed_refs, slots_refs, refs = refs[:2], refs[2:4], refs[4:]
    turned_ref, targets, out_refs = refs[0], refs[1 : 1 + count], refs[1 + count : -2]
    held_ref, sems = refs[-2:]
    pieces, rows, _ = held_ref.shape
    copies = [
        pltpu.make_async_copy(in_ref.at[pl.ds(k * rows, rows)], held_ref.at[k], sems.at[k])
        for k in range(pieces)
    ]
    others = [
        pltpu.make_async_copy(source, target, sems.at[pieces + k])
        for k, (source, target) in enumerate(zip(sources, targets))
    ]
    for copy in copies + others:
        copy.start()
    for part, (normed_ref, slots_ref) in enumerate(zip(normed_refs, slots_refs)):
        packed = picked(section_ref[0], slots_ref[...], normed_ref[...], steps, per_expert)
        each = packed.shape[0] // len(steps)
        for place, out_ref in enumerate(out_refs):
            out_ref[part * each : (part + 1) * each, :] = packed[
                place * each : (place + 1) * each, :
            ]
    for k in range(pieces):
        copies[k].wait()
        turned_ref[:, k * rows : (k + 1) * rows] = held_ref[k].T
    for copy in others:
        copy.wait()


def load_weights(section, stacked_in, others, normed, slots, steps, per_expert):
    count = len(others)
    rows, width = stacked_in.shape
    pieces = max(1, rows // LANES)
    arrays = [pltpu.with_memory_space_constraint(a, pltpu.HBM) for a in (stacked_in, *others)]
    shapes = [shaped(width, rows, stacked_in.dtype)]
    shapes += [jax.ShapeDtypeStruct(a.shape, a.dtype) for a in others]
    shapes += [shaped(normed[0].shape[0], width, jnp.bfloat16)] * len(steps)
    return pl.pallas_call(
        functools.partial(load_kernel, count, steps, per_expert),
        out_shape=shapes,
        in_specs=[SMEM] + [HBM] * (count + 1) + [VMEM] * 4,
        out_specs=[VMEM] * len(shapes),
        scratch_shapes=[
            pltpu.VMEM((pieces, rows // pieces, width), stacked_in.dtype),
            pltpu.SemaphoreType.DMA((pieces + count,)),
        ],
        compiler_params=PARAMS,
        name="load_weights",
    )(section, *arrays, *normed, *slots)


def expert_kernel(count, after, in_ref, down_ref, *refs):
    blocks, every_ref = refs[:count], refs[-1]
    out_refs = refs[count + after : -1]
    every = gathered(blocks, every_ref)
    gate_up = jnp.dot(every, in_ref[...], preferred_element_type=jnp.float32)
    hidden = gate_up.shape[1] // 2
    gate = gate_up[:, :hidden]
    active = (gate / (1.0 + jnp.exp(-gate)) * gate_up[:, hidden:]).astype(jnp.bfloat16)
    partial = jnp.dot(active, down_ref[...], preferred_element_type=jnp.float32)
    rows = out_refs[0].shape[0]
    for place, out_ref in enumerate(out_refs):
        out_ref[...] = partial[place * rows : (place + 1) * rows, :].astype(jnp.bfloat16)


def run_expert(blocks, turned_in, down, pieces, after=()):
    count = len(blocks)
    rows, width = blocks[0].shape
    return pl.pallas_call(
        functools.partial(expert_kernel, count, len(after)),
        out_shape=[shaped(rows // pieces, width, jnp.bfloat16)] * (count * pieces),
        in_specs=[VMEM] * (2 + count) + [ANY] * len(after),
        out_specs=[VMEM] * (count * pieces),
        scratch_shapes=[pltpu.VMEM((count * rows, width), jnp.bfloat16)],
        compiler_params=PARAMS,
        name="expert",
    )(turned_in, down, *blocks, *after)


def gathered(blocks, every_ref):
    rows = blocks[0].shape[0]
    for place, block in enumerate(blocks):
        every_ref[place * rows : (place + 1) * rows, :] = block[...]
    return every_ref[...]


def add_kernel(count, high_ref, low_ref, begun_ref, *refs):
    blocks, out_ref, every_ref = refs[:count], refs[count], refs[-1]
    every = gathered(blocks, every_ref)
    total = begun_ref[...] + jnp.dot(low_ref[...], every, preferred_element_type=jnp.float32)
    out_ref[...] = total + jnp.dot(high_ref[...], every, preferred_element_type=jnp.float32)


def add_to(high, low, begun, blocks):
    count = len(blocks)
    each, width = blocks[0].shape
    return pl.pallas_call(
        functools.partial(add_kernel, count),
        out_shape=shaped(*begun.shape, jnp.float32),
        in_specs=[VMEM] * (3 + count),
        out_specs=VMEM,
        scratch_shapes=[pltpu.VMEM((count * each, width), jnp.bfloat16)],
        compiler_params=PARAMS,
        name="add_to",
    )(high, low, begun, *blocks)


def begin_kernel(count, high_ref, low_ref, *refs):
    blocks, out_ref, every_ref = refs[:count], refs[count], refs[-1]
    every = gathered(blocks, every_ref)
    total = jnp.dot(low_ref[...], every, preferred_element_type=jnp.float32)
    out_ref[...] = total + jnp.dot(high_ref[...], every, preferred_element_type=jnp.float32)


def begin(high, low, blocks):
    count = len(blocks)
    each, width = blocks[0].shape
    return pl.pallas_call(
        functools.partial(begin_kernel, count),
        out_shape=shaped(high.shape[0], width, jnp.float32),
        in_specs=[VMEM] * (2 + count),
        out_specs=VMEM,
        scratch_shapes=[pltpu.VMEM((count * each, width), jnp.bfloat16)],
        compiler_params=PARAMS,
        name="begin",
    )(high, low, *blocks)


def close_kernel(count, targets, member_ref, tokens_ref, high_ref, low_ref, begun_ref, *refs):
    blocks, outs, every_ref, total_ref = refs[:count], refs[count:-2], refs[-2], refs[-1]
    every = gathered(blocks, every_ref)
    total = begun_ref[...] + jnp.dot(low_ref[...], every, preferred_element_type=jnp.float32)
    total_ref[...] = total + jnp.dot(high_ref[...], every, preferred_element_type=jnp.float32)
    if len(outs) == 1:
        outs[0][...] = total_ref[...]
        return
    part = outs[0].shape[1]
    for k, out_ref in enumerate(outs):
        place = target_of(member_ref[0], targets[k - 1]) if k else member_ref[0]
        columns = pl.ds(pl.multiple_of(place * part, LANES), part)
        value = total_ref[:, columns]
        if k == 0:
            value = value + tokens_ref[:, columns].astype(jnp.float32)
        out_ref[...] = value.astype(out_ref.dtype)


def close(high, low, begun, blocks, tokens, member, inner_count):
    count = len(blocks)
    each = blocks[0].shape[0]
    rows, width = begun.shape
    part = width // inner_count
    whole = part % LANES != 0
    targets = inner_targets(inner_count)
    kinds = [jnp.float32] + [jnp.bfloat16] * (inner_count - 1)
    shapes = [shaped(rows, part, kind) for kind in kinds]
    if whole:
        shapes = [shaped(rows, width, jnp.float32)]
    outs = pl.pallas_call(
        functools.partial(close_kernel, count, targets),
        out_shape=shapes,
        in_specs=[SMEM] + [VMEM] * (4 + count),
        out_specs=[VMEM] * len(shapes),
        scratch_shapes=[
            pltpu.VMEM((count * each, width), jnp.bfloat16),
            pltpu.VMEM((rows, width), jnp.float32),
        ],
        compiler_params=PARAMS,
        name="close",
    )(member.reshape(1), tokens, high, low, begun, *blocks)
    if not whole:
        return outs
    rounded = outs[0].astype(jnp.bfloat16)
    total = outs[0] + tokens.astype(jnp.float32)
    outs = [lax.dynamic_slice_in_dim(total, member * part, part, 1)]
    for k in range(1, inner_count):
        place = target_of(member, targets[k - 1])
        outs.append(lax.dynamic_slice_in_dim(rounded, place * part, part, 1))
    return outs


def final_kernel(*refs):
    out_ref = refs[-1]
    micro, row_count, _ = out_ref.shape
    total = refs[0][...]
    for ref in refs[1:-1]:
        total = total + ref[...].astype(jnp.float32)
    for m in range(micro):
        out_ref[m] = total[m * row_count : (m + 1) * row_count].astype(out_ref.dtype)


def finish(pieces, micro, row_count):
    part = pieces[0].shape[1]
    return pl.pallas_call(
        final_kernel,
        out_shape=jax.ShapeDtypeStruct((micro, row_count, part), jnp.bfloat16),
        in_specs=[VMEM] * len(pieces),
        out_specs=VMEM,
        compiler_params=PARAMS,
        name="finish",
    )(*pieces)


def body(tokens, norm_gain, router, expert_in, expert_out, choices):
    sections = lax.axis_size("section")
    inner_count = lax.axis_size("inner")
    member = lax.axis_index("inner").astype(jnp.int32)
    section = lax.axis_index("section").astype(jnp.int32).reshape(1)
    chips = sections // 2
    experts = router.shape[1]
    per_expert = sections // experts
    micro, row_count, width = tokens.shape
    rows = micro * row_count
    hidden = expert_in.shape[2]
    own = tokens.reshape(rows, width)
    named = choices.transpose(0, 2, 1)
    gain = norm_gain.reshape(1, width)

    far = chips - 1
    first_steps = ((0, 0), (far, far))
    steps = []
    for k in range(1, far, 2):
        steps += [(k, k + 1), (k + 1, k)]

    other = trade(own, "section", 1)
    other_named = trade(named, "section", 1)
    *halves, own, gain, normed, slots, names = own_part(
        section, own, named, gain, first_steps, per_expert, experts
    )
    message, away, other_normed, other_slots = other_part(
        section, other, other_named, gain, halves, first_steps, per_expert, experts
    )
    away = visit(away, (far, far), 0)
    turned_in, router_rows, down, *messages = load_weights(
        section,
        expert_in[0].reshape(2 * hidden, width),
        (router.T, expert_out[0]),
        (normed, other_normed),
        (slots, other_slots),
        tuple(steps),
        per_expert,
    )
    arrived = [visit(value, step, 0) for value, step in zip(messages, steps)]

    def origins(step):
        a, b = step
        return ((2 * a, 2 * b), (2 * b + 1, 2 * a + 1))

    early = origins((far, far)) + origins((0, 0))
    late = tuple(pair for step in steps for pair in origins(step))
    sets = (early, late[:2], late[2:])
    high_a, low_a, high_m, low_m, high_b, low_b = mix(
        section, normed, slots, names, router_rows, sets, per_expert
    )
    here, beside = run_expert([message], turned_in, down, 2)
    beside = trade(beside, "section", 1)
    away = run_expert([away], turned_in, down, 2, (here,))
    results = run_expert(arrived, turned_in, down, 2, (away[0],))
    away = [visit(value, (far, far), cross) for cross, value in enumerate(away)]
    begun = begin(high_a, low_a, [*away, here, beside])
    results = [visit(value, steps[j // 2], j % 2) for j, value in enumerate(results)]
    begun = add_to(high_m, low_m, begun, results[:2])
    split = close(high_b, low_b, begun, results[2:], own, member, inner_count)
    targets = inner_targets(inner_count)
    pieces = [split[0]] + [turn(value, order) for value, order in zip(split[1:], targets)]
    return finish(pieces, micro, row_count)


def solution(mesh):
    return jax.shard_map(
        body,
        mesh=mesh,
        in_specs=(
            P(None, "section", None),
            P(),
            P(),
            P("section", None, "inner", None),
            P("section", "inner", None),
            P(None, "section", None),
        ),
        out_specs=P(None, "section", "inner"),
        check_vma=False,
    )
```

```python
import functools

import jax
import jax.numpy as jnp
from jax import lax
from jax.experimental import pallas as pl
from jax.experimental.pallas import tpu as pltpu
from jax.sharding import PartitionSpec as P

epsilon = 1e-05
LANES = 128
FIRST = (0,)
INNER_STEPS = ((1, 1), (2, 2), (3, 3))
TOKEN_COPIES = 4
NT = (((1,), (1,)), ((), ()))
VMEM = pl.BlockSpec(memory_space=pltpu.VMEM)
ANY = pl.BlockSpec(memory_space=pl.ANY)
HBM = pl.BlockSpec(memory_space=pltpu.HBM)
SMEM = pl.BlockSpec(memory_space=pltpu.SMEM)
PARAMS = pltpu.CompilerParams(vmem_limit_bytes=20 * 1024 * 1024)


def trade(value, axis, distance):
    count = lax.axis_size(axis)
    return lax.ppermute(value, axis, [(place, place ^ distance) for place in range(count)])


def inner_steps(count):
    if count == len(INNER_STEPS) + 1:
        return INNER_STEPS
    return tuple((k, k) for k in range(1, count))


def place_after(member, section, step, count):
    return lax.rem(member + jnp.where(section % 2 == 0, step[0], step[1]), count)


def turn(value, step):
    sections, count = lax.axis_size("section"), lax.axis_size("inner")
    pairs = [
        (section * count + place, section * count + (place + step[section % 2]) % count)
        for section in range(sections)
        for place in range(count)
    ]
    return lax.ppermute(value, ("section", "inner"), pairs)


def visit(value, step, cross):
    count = lax.axis_size("section")
    pairs = [(place, place ^ (2 * step[place % 2]) ^ cross) for place in range(count)]
    return lax.ppermute(value, "section", pairs)


def shaped(rows, width, dtype):
    return jax.ShapeDtypeStruct((rows, width), dtype)


def expert_at(section, distances, per_expert):
    distance = jnp.where(section % 2 == 0, distances[0], distances[1])
    return lax.div(section ^ distance, jnp.int32(per_expert)).astype(jnp.float32)


def slots_of(named, experts, row_count):
    rows = named[0].shape[1]
    ids = lax.broadcasted_iota(jnp.int32, (experts, rows), 0).astype(jnp.float32)
    hit = (named[0] == ids) | (named[1] == ids)
    above = lax.broadcasted_iota(jnp.int32, (rows, rows), 0)
    column = lax.broadcasted_iota(jnp.int32, (rows, rows), 1)
    earlier = (above < column) & (above // row_count == column // row_count)
    rank = jnp.dot(
        hit.astype(jnp.bfloat16), earlier.astype(jnp.bfloat16), preferred_element_type=jnp.float32
    )
    group = lax.broadcasted_iota(jnp.int32, (experts, rows), 1) // row_count
    return jnp.where(hit, (group * (row_count // 2)).astype(jnp.float32) + rank, -1.0)


def picked(section, slots, normed, steps, per_expert):
    experts, rows = slots.shape
    ids = lax.broadcasted_iota(jnp.int32, (experts, rows), 0).astype(jnp.float32)
    slot_ids = lax.broadcasted_iota(jnp.int32, (rows // 2, rows), 0).astype(jnp.float32)
    picks = []
    for step in steps:
        expert = expert_at(section, (2 * step[0], 2 * step[1]), per_expert)
        slot = jnp.sum(jnp.where(ids == expert, slots, 0.0), axis=0, keepdims=True)
        picks.append(jnp.where(slot == slot_ids, 1.0, 0.0))
    pick = jnp.concatenate(picks, axis=0).astype(jnp.bfloat16)
    return jnp.dot(pick, normed, preferred_element_type=jnp.float32).astype(jnp.bfloat16)


def normed_of(values, gain):
    values = values.astype(jnp.float32)
    inv_rms = lax.rsqrt(jnp.mean(values * values, axis=-1, keepdims=True) + epsilon)
    return (values * inv_rms * gain).astype(jnp.bfloat16)


def named_of(ref):
    micro = ref.shape[0]
    return [
        jnp.concatenate([ref[m, k : k + 1, :] for m in range(micro)], axis=1).astype(jnp.float32)
        for k in range(2)
    ]


def own_kernel(steps, per_expert, section_ref, tokens_ref, named_ref, gain_ref, *refs):
    half_refs, refs = refs[: len(steps)], refs[len(steps) :]
    own_ref, gain_out_ref, normed_ref, slots_ref, names_ref, held_ref, sems = refs
    width = tokens_ref.shape[1]
    chunk = width // TOKEN_COPIES
    spans = [pl.ds(k * chunk, chunk) for k in range(TOKEN_COPIES)]
    pairs = [(tokens_ref.at[:, span], own_ref.at[:, span]) for span in spans]
    pairs = [(named_ref, held_ref), *pairs, (gain_ref, gain_out_ref)]
    copies = [
        pltpu.make_async_copy(source, target, sems.at[k])
        for k, (source, target) in enumerate(pairs)
    ]
    for copy in copies:
        copy.start()
    copies[0].wait()
    named = named_of(held_ref)
    slots = slots_of(named, slots_ref.shape[0], named_ref.shape[2])
    slots_ref[...] = slots
    names_ref[0:1, :] = named[0]
    names_ref[1:2, :] = named[1]
    for copy in copies[1:]:
        copy.wait()
    normed = normed_of(own_ref[...], gain_out_ref[...])
    normed_ref[...] = normed
    packed = picked(section_ref[0], slots, normed, steps, per_expert)
    each = packed.shape[0] // len(steps)
    for place, half_ref in enumerate(half_refs):
        half_ref[...] = packed[place * each : (place + 1) * each, :]


def own_part(section, tokens, named, gain, steps, per_expert, experts):
    rows, width = tokens.shape
    arrays = [pltpu.with_memory_space_constraint(a, pltpu.HBM) for a in (tokens, named, gain)]
    shapes = [shaped(rows // 2, width, jnp.bfloat16)] * len(steps) + [
        shaped(rows, width, jnp.bfloat16),
        shaped(1, width, jnp.float32),
        shaped(rows, width, jnp.bfloat16),
        shaped(experts, rows, jnp.float32),
        shaped(2, rows, jnp.float32),
    ]
    return pl.pallas_call(
        functools.partial(own_kernel, steps, per_expert),
        out_shape=shapes,
        in_specs=[SMEM] + [HBM] * 3,
        out_specs=[VMEM] * len(shapes),
        scratch_shapes=[pltpu.VMEM(named.shape, jnp.int32), pltpu.SemaphoreType.DMA((TOKEN_COPIES + 2,))],
        compiler_params=PARAMS,
        name="own_part",
    )(section, *arrays)


def other_kernel(steps, per_expert, section_ref, other_ref, named_ref, gain_ref, *refs):
    count = len(steps)
    half_refs, out_refs, normed_ref, slots_ref = refs[:count], refs[count:-2], refs[-2], refs[-1]
    slots = slots_of(named_of(named_ref), slots_ref.shape[0], named_ref.shape[2])
    slots_ref[...] = slots
    normed = normed_of(other_ref[...], gain_ref[...])
    normed_ref[...] = normed
    packed = picked(section_ref[0], slots, normed, steps, per_expert)
    each = packed.shape[0] // count
    for place, (half_ref, out_ref) in enumerate(zip(half_refs, out_refs)):
        out_ref[:each, :] = half_ref[...]
        out_ref[each:, :] = packed[place * each : (place + 1) * each, :]


def other_part(section, other, named, gain, halves, steps, per_expert, experts):
    rows, width = other.shape
    shapes = [shaped(rows, width, jnp.bfloat16)] * (len(steps) + 1)
    shapes.append(shaped(experts, rows, jnp.float32))
    return pl.pallas_call(
        functools.partial(other_kernel, steps, per_expert),
        out_shape=shapes,
        in_specs=[SMEM] + [VMEM] * (3 + len(halves)),
        out_specs=[VMEM] * len(shapes),
        compiler_params=PARAMS,
        name="other_part",
    )(section, other, named, gain, *halves)


def mix_kernel(sets, per_expert, section_ref, normed_ref, slots_ref, named_ref, router_ref, *outs):
    experts, every = slots_ref.shape
    logits = lax.dot_general(
        normed_ref[...], router_ref[...], NT, preferred_element_type=jnp.float32
    )
    diagonal = lax.broadcasted_iota(jnp.int32, (every, every), 0) == (
        lax.broadcasted_iota(jnp.int32, (every, every), 1)
    )

    def upright(row):
        return jnp.sum(jnp.where(diagonal, row, 0.0), axis=1, keepdims=True)

    first, second = upright(named_ref[0:1, :]), upright(named_ref[1:2, :])
    ids = lax.broadcasted_iota(jnp.int32, logits.shape, 1).astype(jnp.float32)
    lead = jnp.sum(jnp.where(first == ids, logits, 0.0), axis=1, keepdims=True)
    trail = jnp.sum(jnp.where(second == ids, logits, 0.0), axis=1, keepdims=True)
    weight_a = 1.0 / (1.0 + jnp.exp(trail - lead))
    weight_b = 1.0 / (1.0 + jnp.exp(lead - trail))
    section = section_ref[0]
    tall = lax.broadcasted_iota(jnp.int32, (experts, every), 0).astype(jnp.float32)
    for place, distances in enumerate(sets):
        out_ref = outs[place]
        count, width = out_ref.shape[0], out_ref.shape[1] // 2
        each = width // len(distances)
        lanes = lax.broadcasted_iota(jnp.int32, (count, width), 1).astype(jnp.float32)
        spread = jnp.zeros((count, width), jnp.float32)
        for at, distance in enumerate(distances):
            expert = expert_at(section, distance, per_expert)
            slot = jnp.sum(jnp.where(tall == expert, slots_ref[...], 0.0), axis=0, keepdims=True)
            weight = jnp.where(first == expert, weight_a, 0.0) + jnp.where(
                second == expert, weight_b, 0.0
            )
            spread = spread + jnp.where(
                upright(slot) + at * each == lanes, weight, 0.0
            )
        high = spread.astype(jnp.bfloat16)
        low = (spread - high.astype(jnp.float32)).astype(jnp.bfloat16)
        out_ref[...] = jnp.concatenate([high, low], axis=1)


def mix(section, normed, slots, named, router, early, near, per_expert):
    rows = normed.shape[0]
    shapes = [
        shaped(rows, len(distances) * rows, jnp.bfloat16) for distances in (early, near)
    ]
    return pl.pallas_call(
        functools.partial(mix_kernel, (early, near), per_expert),
        out_shape=shapes,
        in_specs=[SMEM] + [VMEM] * 4,
        out_specs=[VMEM] * len(shapes),
        compiler_params=PARAMS,
        name="mix",
    )(section, normed, slots, named, router)


def near_kernel(steps, per_expert, section_ref, *refs):
    normed_refs, slots_refs, out_refs = refs[:2], refs[2:4], refs[5:]
    for part in range(2):
        packed = picked(
            section_ref[0], slots_refs[part][...], normed_refs[part][...], steps, per_expert
        )
        each = packed.shape[0] // len(steps)
        for place, out_ref in enumerate(out_refs):
            out_ref[part * each : (part + 1) * each, :] = packed[
                place * each : (place + 1) * each, :
            ]


def pack_near(section, normed, slots, steps, per_expert, after):
    rows, width = normed[0].shape
    return pl.pallas_call(
        functools.partial(near_kernel, steps, per_expert),
        out_shape=[shaped(rows, width, jnp.bfloat16)] * len(steps),
        in_specs=[SMEM] + [VMEM] * 4 + [ANY],
        out_specs=[VMEM] * len(steps),
        compiler_params=PARAMS,
        name="pack_near",
    )(section, *normed, *slots, after)


def load_kernel(count, steps, per_expert, section_ref, in_ref, *refs):
    sources, refs = refs[:count], refs[count:]
    normed_refs, slots_refs, refs = refs[:2], refs[2:4], refs[4:]
    turned_ref, targets, out_refs = refs[0], refs[1 : 1 + count], refs[1 + count : -2]
    held_ref, sems = refs[-2:]
    pieces, rows, _ = held_ref.shape
    copies = [
        pltpu.make_async_copy(in_ref.at[pl.ds(k * rows, rows)], held_ref.at[k], sems.at[k])
        for k in range(pieces)
    ]
    others = [
        pltpu.make_async_copy(source, target, sems.at[pieces + k])
        for k, (source, target) in enumerate(zip(sources, targets))
    ]
    for copy in copies + others:
        copy.start()
    for part, (normed_ref, slots_ref) in enumerate(zip(normed_refs, slots_refs)):
        if not steps:
            break
        packed = picked(section_ref[0], slots_ref[...], normed_ref[...], steps, per_expert)
        each = packed.shape[0] // len(steps)
        for place, out_ref in enumerate(out_refs):
            out_ref[part * each : (part + 1) * each, :] = packed[
                place * each : (place + 1) * each, :
            ]
    for k in range(pieces):
        copies[k].wait()
        turned_ref[:, k * rows : (k + 1) * rows] = held_ref[k].T
    for copy in others:
        copy.wait()


def load_weights(section, stacked_in, others, normed, slots, steps, per_expert):
    count = len(others)
    rows, width = stacked_in.shape
    pieces = max(1, rows // LANES)
    arrays = [pltpu.with_memory_space_constraint(a, pltpu.HBM) for a in (stacked_in, *others)]
    shapes = [shaped(width, rows, stacked_in.dtype)]
    shapes += [jax.ShapeDtypeStruct(a.shape, a.dtype) for a in others]
    shapes += [shaped(normed[0].shape[0], width, jnp.bfloat16)] * len(steps)
    return pl.pallas_call(
        functools.partial(load_kernel, count, steps, per_expert),
        out_shape=shapes,
        in_specs=[SMEM] + [HBM] * (count + 1) + [VMEM] * 4,
        out_specs=[VMEM] * len(shapes),
        scratch_shapes=[
            pltpu.VMEM((pieces, rows // pieces, width), stacked_in.dtype),
            pltpu.SemaphoreType.DMA((pieces + count,)),
        ],
        compiler_params=PARAMS,
        name="load_weights",
    )(section, *arrays, *normed, *slots)


def expert_kernel(count, after, in_ref, down_ref, *refs):
    blocks, every_ref = refs[:count], refs[-1]
    out_refs = refs[count + after : -1]
    every = gathered(blocks, every_ref)
    gate_up = jnp.dot(every, in_ref[...], preferred_element_type=jnp.float32)
    hidden = gate_up.shape[1] // 2
    gate = gate_up[:, :hidden]
    active = (gate / (1.0 + jnp.exp(-gate)) * gate_up[:, hidden:]).astype(jnp.bfloat16)
    partial = jnp.dot(active, down_ref[...], preferred_element_type=jnp.float32)
    rows = out_refs[0].shape[0]
    for place, out_ref in enumerate(out_refs):
        out_ref[...] = partial[place * rows : (place + 1) * rows, :].astype(jnp.bfloat16)


def run_expert(blocks, turned_in, down, pieces, after=()):
    count = len(blocks)
    rows, width = blocks[0].shape
    return pl.pallas_call(
        functools.partial(expert_kernel, count, len(after)),
        out_shape=[shaped(rows // pieces, width, jnp.bfloat16)] * (count * pieces),
        in_specs=[VMEM] * (2 + count) + [ANY] * len(after),
        out_specs=[VMEM] * (count * pieces),
        scratch_shapes=[pltpu.VMEM((count * rows, width), jnp.bfloat16)],
        compiler_params=PARAMS,
        name="expert",
    )(turned_in, down, *blocks, *after)


def gathered(blocks, every_ref):
    rows = blocks[0].shape[0]
    for place, block in enumerate(blocks):
        every_ref[place * rows : (place + 1) * rows, :] = block[...]
    return every_ref[...]


def weighed(weights_ref, blocks, every_ref):
    gathered((*blocks, *blocks), every_ref)
    return jnp.dot(weights_ref[...], every_ref[...], preferred_element_type=jnp.float32)


def begin_kernel(count, weights_ref, *refs):
    blocks, out_ref, every_ref = refs[:count], refs[count], refs[-1]
    out_ref[...] = weighed(weights_ref, blocks, every_ref)


def begin(weights, blocks):
    count = len(blocks)
    each, width = blocks[0].shape
    return pl.pallas_call(
        functools.partial(begin_kernel, count),
        out_shape=shaped(weights.shape[0], width, jnp.float32),
        in_specs=[VMEM] * (1 + count),
        out_specs=VMEM,
        scratch_shapes=[pltpu.VMEM((2 * count * each, width), jnp.bfloat16)],
        compiler_params=PARAMS,
        name="begin",
    )(weights, *blocks)


def close_kernel(count, steps, member_ref, section_ref, tokens_ref, weights_ref, begun_ref, *refs):
    blocks, outs, every_ref, total_ref = refs[:count], refs[count:-2], refs[-2], refs[-1]
    total_ref[...] = begun_ref[...] + weighed(weights_ref, blocks, every_ref)
    if len(outs) == 1:
        outs[0][...] = total_ref[...]
        return
    part = outs[0].shape[1]
    for k, out_ref in enumerate(outs):
        place = member_ref[0]
        if k:
            place = place_after(place, section_ref[0], steps[k - 1], len(outs))
        columns = pl.ds(pl.multiple_of(place * part, LANES), part)
        value = total_ref[:, columns]
        if k == 0:
            value = value + tokens_ref[:, columns].astype(jnp.float32)
        out_ref[...] = value.astype(out_ref.dtype)


def close(weights, begun, blocks, tokens, member, section, inner_count):
    count = len(blocks)
    each = blocks[0].shape[0]
    rows, width = begun.shape
    part = width // inner_count
    whole = part % LANES != 0
    steps = inner_steps(inner_count)
    kinds = [jnp.float32] + [jnp.bfloat16] * (inner_count - 1)
    shapes = [shaped(rows, part, kind) for kind in kinds]
    if whole:
        shapes = [shaped(rows, width, jnp.float32)]
    outs = pl.pallas_call(
        functools.partial(close_kernel, count, steps),
        out_shape=shapes,
        in_specs=[SMEM] * 2 + [VMEM] * (3 + count),
        out_specs=[VMEM] * len(shapes),
        scratch_shapes=[
            pltpu.VMEM((2 * count * each, width), jnp.bfloat16),
            pltpu.VMEM((rows, width), jnp.float32),
        ],
        compiler_params=PARAMS,
        name="close",
    )(member.reshape(1), section, tokens, weights, begun, *blocks)
    if not whole:
        return outs
    rounded = outs[0].astype(jnp.bfloat16)
    total = outs[0] + tokens.astype(jnp.float32)
    outs = [lax.dynamic_slice_in_dim(total, member * part, part, 1)]
    for k in range(1, inner_count):
        place = place_after(member, section[0], steps[k - 1], inner_count)
        outs.append(lax.dynamic_slice_in_dim(rounded, place * part, part, 1))
    return outs


def final_kernel(*refs):
    out_ref = refs[-1]
    micro, row_count, _ = out_ref.shape
    total = refs[0][...]
    for ref in refs[1:-1]:
        total = total + ref[...].astype(jnp.float32)
    for m in range(micro):
        out_ref[m] = total[m * row_count : (m + 1) * row_count].astype(out_ref.dtype)


def finish(pieces, micro, row_count):
    part = pieces[0].shape[1]
    return pl.pallas_call(
        final_kernel,
        out_shape=jax.ShapeDtypeStruct((micro, row_count, part), jnp.bfloat16),
        in_specs=[VMEM] * len(pieces),
        out_specs=VMEM,
        compiler_params=PARAMS,
        name="finish",
    )(*pieces)


def body(tokens, norm_gain, router, expert_in, expert_out, choices):
    sections = lax.axis_size("section")
    inner_count = lax.axis_size("inner")
    member = lax.axis_index("inner").astype(jnp.int32)
    section = lax.axis_index("section").astype(jnp.int32).reshape(1)
    chips = sections // 2
    experts = router.shape[1]
    per_expert = sections // experts
    micro, row_count, width = tokens.shape
    rows = micro * row_count
    hidden = expert_in.shape[2]
    own = tokens.reshape(rows, width)
    named = choices.transpose(0, 2, 1)
    gain = norm_gain.reshape(1, width)

    far = chips - 1
    steps = [(far, far)]
    for k in range(1, far, 2):
        steps += [(k, k + 1), (k + 1, k)]
    first = [steps[k] for k in FIRST]
    second = [step for step in steps if step not in first]
    first_steps = ((0, 0), *first)

    other = trade(own, "section", 1)
    other_named = trade(named, "section", 1)
    *halves, own, gain, normed, slots, names = own_part(
        section, own, named, gain, first_steps, per_expert, experts
    )
    message, *messages, other_normed, other_slots = other_part(
        section, other, other_named, gain, halves, first_steps, per_expert, experts
    )
    first_blocks = [visit(value, step, 0) for value, step in zip(messages, first)]
    turned_in, router_rows, down = load_weights(
        section,
        expert_in[0].reshape(2 * hidden, width),
        (router.T, expert_out[0]),
        (normed, other_normed),
        (slots, other_slots),
        (),
        per_expert,
    )
    messages = pack_near(
        section, (normed, other_normed), (slots, other_slots), tuple(second), per_expert, down
    )
    second_blocks = [visit(value, step, 0) for value, step in zip(messages, second)]

    def origins(step):
        a, b = step
        return ((2 * a, 2 * b), (2 * b + 1, 2 * a + 1))

    def send_back(results, steps):
        return [visit(value, steps[j // 2], j % 2) for j, value in enumerate(results)]

    early = tuple(pair for step in (*first, (0, 0)) for pair in origins(step))
    late = tuple(pair for step in second for pair in origins(step))
    early_weights, late_weights = mix(
        section, normed, slots, names, router_rows, early, late, per_expert
    )
    here, beside = run_expert([message], turned_in, down, 2)
    beside = trade(beside, "section", 1)
    first_results = run_expert(first_blocks, turned_in, down, 2, (here,))
    second_results = run_expert(
        second_blocks, turned_in, down, 2, (first_results[0], beside)
    )
    begun = begin(early_weights, [*send_back(first_results, first), here, beside])
    split = close(
        late_weights,
        begun,
        send_back(second_results, second),
        own,
        member,
        section,
        inner_count,
    )
    pieces = [split[0]]
    pieces += [turn(value, step) for value, step in zip(split[1:], inner_steps(inner_count))]
    return finish(pieces, micro, row_count)


def solution(mesh):
    return jax.shard_map(
        body,
        mesh=mesh,
        in_specs=(
            P(None, "section", None),
            P(),
            P(),
            P("section", None, "inner", None),
            P("section", "inner", None),
            P(None, "section", None),
        ),
        out_specs=P(None, "section", "inner"),
        check_vma=False,
    )
```
